32 devices in a mesh: groups: 2 (over y), row: 4 (over z), col: 4 (over x, core).
Axes of the slice: x: 2, y: 2, z: 4, core: 2. Of those that a mesh axis runs over, the one named last changes fastest.
Arguments:
- acq_data: bfloat16 [12288, 4, 3072], P(('groups', 'row', 'col')), parts along dimension 0, may hold values from -6 to 6
- grid_row: int32 [12288], P(('groups', 'row', 'col')), parts along dimension 0, may hold values from 0 to 3071, as said below
- counts: int32 [32], P(('groups', 'row', 'col')), parts along dimension 0, may hold values from 0 to 384, as said below
Outputs:
- multiples: bfloat16 [4, 4, 3072, 3072], P('groups', None, 'row', 'col'), parts along dimension 0
The draws below stay inside these ranges and needn't reach their ends.
There are 2 independent parts, one for each index of `groups`. The reference program is written for one: setup_inputs(seed, part) draws one part's arguments, and reference() takes and returns one part's arrays. A program takes and returns all parts, laid end to end along the dimension named above; each array names one. Nothing has to cross between parts.
Inputs may be any that keep to these rules, and one draw needn't show every extreme that they name: Over the live slots of all owners grid_row takes every value from 0 to 3071 exactly once; entries of slots that are not live are arbitrary values in the range. Of one owner's live slots at most 96 fall into one block of 768 consecutive grid rows; in each block exactly 4 owners have 96 there, and one owner has 96 in every block. The counts add up to 3072; the largest equals 384. `acq_data`: rows of slots that are not live carry no meaning.
All inputs are finite; a program needn't handle non-finite values.
Results may differ from the reference program's by a relative error of at most 0.004.
Values may be sent and summed in bfloat16 or wider, within the bound.
No kernel may reach another device: no remote copies, remote signals or barrier semaphores. Data moves between devices by JAX's collectives and lax.ppermute only.
A program may use at most 192 MiB of HBM per device.

```python
import math
import jax
import jax.numpy as jnp

NS = 3072
FREQ = 2
ORDERS = 2
PLANES = 4
BLOCK = 768
OWNERS = 16
CAP = 96
SHARE = 4
OWN_CAP = 384
ACQ = 6144


def binning_plan(key):
    key_owner, key_order, key_rows, key_slots = jax.random.split(key, 4)
    block_count = NS // BLOCK
    owner_ids = jnp.arange(OWNERS, dtype=jnp.int32)
    spare_rows = BLOCK - SHARE * CAP
    others = OWNERS - SHARE
    pattern = jnp.where(owner_ids < SHARE, CAP, spare_rows // others + jnp.where(owner_ids - SHARE < spare_rows % others, 1, 0)).astype(jnp.int32)
    chosen = jax.random.randint(key_owner, (), 0, OWNERS, dtype=jnp.int32)
    owner_orders = jax.vmap(lambda sub_key: jax.random.permutation(sub_key, OWNERS))(jax.random.split(key_order, block_count)).astype(jnp.int32)
    leading = owner_orders[:, :1]
    owner_orders = jnp.where(owner_orders == chosen, leading, owner_orders)
    owner_orders = owner_orders.at[:, 0].set(chosen)
    bounds = jnp.cumsum(pattern)
    position = jnp.arange(BLOCK, dtype=jnp.int32)
    owner_slot = jnp.sum((bounds[None, :] <= position[:, None]).astype(jnp.int32), axis=1)
    row_owner = owner_orders[:, owner_slot]
    row_perm = jax.vmap(lambda sub_key: jax.random.permutation(sub_key, BLOCK))(jax.random.split(key_rows, block_count)).astype(jnp.int32)
    grid_rows = (jnp.arange(block_count, dtype=jnp.int32)[:, None] * BLOCK + row_perm).reshape(-1)
    owner_flat = row_owner.reshape(-1)
    shuffle = jax.random.permutation(key_slots, NS).astype(jnp.int32)
    order_of_rows = jnp.argsort(owner_flat * NS + shuffle, stable=True)
    counts = jnp.sum((owner_flat[:, None] == owner_ids[None, :]).astype(jnp.int32), axis=0)
    starts = jnp.cumsum(counts) - counts
    sorted_owner = owner_flat[order_of_rows]
    within = jnp.arange(NS, dtype=jnp.int32) - starts[sorted_owner]
    slot_of = sorted_owner * OWN_CAP + within
    return (grid_rows[order_of_rows], slot_of, counts)


def draw_grid_row(key, part):
    placed_rows, slot_of, counts = binning_plan(key)
    key = jax.random.fold_in(key, 5)
    filler = jax.random.randint(key, (ACQ,), 0, NS, dtype=jnp.int32)
    return filler.at[slot_of].set(placed_rows)


def draw_counts(key, part):
    placed_rows, slot_of, counts = binning_plan(key)
    return counts


def levels(rng, shape, shards, smallest, high):
    level = 1.0
    for axis_at, shards_of in shards:
        steps = jax.random.uniform(jax.random.fold_in(jax.random.fold_in(rng, 6), axis_at), (shards_of,), jnp.float32, smallest / len(shards), high / len(shards))
        level = level * jnp.repeat(jnp.exp(steps), shape[axis_at] // shards_of).reshape((-1,) + (1,) * (len(shape) - 1 - axis_at))
    return level


def normal_values(own_key, dims, deviation, limit, shards=(), kind=jnp.bfloat16):
    factor_of = levels(own_key, dims, shards, -0.22, 0.18) if shards else 1.0
    array = jax.random.normal(own_key, dims, jnp.float32) * deviation * factor_of
    return jnp.minimum(jnp.maximum(array, -limit), limit).astype(kind)


def setup_inputs(seed: int = 0, part: int = 0) -> dict:
    key_list = jax.random.split(jax.random.key(seed), 4)
    own_keys = jax.random.split(jax.random.fold_in(key_list[3], part), 4)
    return {
        "acq_data": normal_values(own_keys[0], (ACQ, PLANES, NS), 1.0, 6.0, ((0, 16),)),
        "grid_row": draw_grid_row(jax.random.fold_in(jax.random.fold_in(key_list[3], part), 71), part),
        "counts": draw_counts(jax.random.fold_in(jax.random.fold_in(key_list[3], part), 71), part),
    }


def reference(acq_data, grid_row, counts):
    slot_index = jnp.arange(ACQ, dtype=jnp.int32)
    owner_index = (slot_index // OWN_CAP).astype(jnp.int32)
    live_slot = slot_index % OWN_CAP < counts[owner_index]
    target_row = jnp.where(live_slot, grid_row, NS).astype(jnp.int32)
    binned = jnp.zeros((NS, PLANES, NS), acq_data.dtype).at[target_row].set(acq_data, mode='drop')
    grid_field = jnp.transpose(binned, (1, 0, 2))
    weight = 1.0 / math.sqrt(2.0 * NS)
    results = []
    current = grid_field
    for order_index in range(ORDERS):
        new_planes = []
        for freq_index in range(FREQ):
            prior_real = current[2 * freq_index]
            prior_imag = current[2 * freq_index + 1]
            data_real = grid_field[2 * freq_index]
            data_imag = grid_field[2 * freq_index + 1]
            real_part = jnp.dot(prior_real, data_real, preferred_element_type=jnp.float32) - jnp.dot(prior_imag, data_imag, preferred_element_type=jnp.float32)
            imag_part = jnp.dot(prior_real, data_imag, preferred_element_type=jnp.float32) + jnp.dot(prior_imag, data_real, preferred_element_type=jnp.float32)
            new_planes.append((real_part * weight).astype(jnp.bfloat16))
            new_planes.append((imag_part * weight).astype(jnp.bfloat16))
        current = jnp.stack(new_planes, axis=0)
        results.append(current)
    return jnp.stack(results, axis=0)
```

```python
import functools
import math

import jax
import jax.numpy as jnp
from jax import lax
from jax.experimental import pallas as pl
from jax.experimental.pallas import tpu as pltpu
from jax.sharding import PartitionSpec as P

NS = 3072
ORDERS = 2
FREQ = 2
THIRDS = 3
BF16 = jnp.bfloat16
F32 = jnp.float32


def bits_of(n_col):
    bit_list = []
    bit = n_col // 2
    while bit:
        bit_list.append(bit)
        bit //= 2
    return bit_list


def gather_cols(piece, n_col):
    held = {0: piece}
    for bit in bits_of(n_col):
        pairs = [(c, c ^ bit) for c in range(n_col)]
        arrived = {d ^ bit: lax.ppermute(a, "col", pairs) for d, a in held.items()}
        held.update(arrived)
    return held


def product_kernel(depths, weight, offs, *refs):
    count = len(depths)
    lefts, right, out = refs[:count], refs[count], refs[count + 1]
    width = right.shape[1] // 2
    rows = out.shape[0]
    by_real = jnp.zeros((rows, 2 * width), F32)
    by_imag = jnp.zeros((rows, 2 * width), F32)
    for i, depth in enumerate(depths):
        start = pl.multiple_of(offs[i], 128)
        block = right[pl.ds(start, depth), :]
        by_real += jnp.dot(lefts[i][:, :depth], block, preferred_element_type=F32)
        by_imag += jnp.dot(lefts[i][:, depth:], block, preferred_element_type=F32)
    real = by_real[:, :width] - by_imag[:, width:]
    imag = by_real[:, width:] + by_imag[:, :width]
    out[:, :width] = (real * weight).astype(BF16)
    out[:, width:] = (imag * weight).astype(BF16)


def complex_product(offs, lefts, right, weight):
    rows = lefts[0].shape[0]
    tile = 256 if rows % 256 == 0 else rows
    depths = [a.shape[1] // 2 for a in lefts]
    wide = right.shape[1]
    spec = pltpu.PrefetchScalarGridSpec(
        num_scalar_prefetch=1,
        grid=(rows // tile,),
        in_specs=[pl.BlockSpec((tile, a.shape[1]), lambda i, s: (i, 0)) for a in lefts]
        + [pl.BlockSpec(right.shape, lambda i, s: (0, 0))],
        out_specs=pl.BlockSpec((tile, wide), lambda i, s: (i, 0)),
    )
    return pl.pallas_call(
        functools.partial(product_kernel, depths, weight),
        grid_spec=spec,
        out_shape=jax.ShapeDtypeStruct((rows, wide), BF16),
        compiler_params=pltpu.CompilerParams(vmem_limit_bytes=40 * 2**20),
        cost_estimate=pl.CostEstimate(
            flops=4 * rows * NS * wide, bytes_accessed=2 * NS * (wide + 2 * rows), transcendentals=0
        ),
    )(offs, *lefts, right)


def per_device(acq_data, grid_row, counts):
    n_row = lax.axis_size("row")
    n_col = lax.axis_size("col")
    own_cap, planes, order = acq_data.shape
    block_rows = order // n_row
    tile_cols = order // n_col
    cap = own_cap // n_row
    slots = n_row * cap
    sub = tile_cols // THIRDS
    weight = 1.0 / math.sqrt(2.0 * NS)
    me = lax.axis_index("col")

    slot_index = jnp.arange(own_cap, dtype=jnp.int32)
    block = jnp.where(slot_index < counts[0], grid_row // block_rows, n_row)
    earlier = (block[None, :] == block[:, None]) & (slot_index[None, :] < slot_index[:, None])
    rank = jnp.sum(earlier.astype(jnp.int32), axis=1)
    leaving = jnp.where(block < n_row, block * cap + rank, -1)
    hit = jnp.arange(slots, dtype=jnp.int32)[:, None] == leaving[None, :]
    spots = jnp.sum(jnp.where(hit, (grid_row % block_rows)[None, :] + 1, 0), axis=1) - 1
    labels = jnp.broadcast_to(spots.reshape(n_row, 1, cap), (n_row, n_col, cap))
    places = lax.all_to_all(
        labels.reshape(n_row * n_col, cap), ("row", "col"), split_axis=0, concat_axis=0, tiled=True
    ).reshape(-1)
    picker = hit.astype(BF16)
    placer = (jnp.arange(block_rows, dtype=jnp.int32)[:, None] == places[None, :]).astype(BF16)

    tiles = []
    for f in range(FREQ):
        raw = acq_data[:, 2 * f : 2 * f + 2, :].reshape(own_cap, 2 * order)
        sent = jnp.dot(picker, raw, preferred_element_type=F32).astype(BF16)
        sent = sent.reshape(n_row, cap, 2, n_col, tile_cols).transpose(0, 3, 1, 2, 4)
        sent = sent.reshape(n_row * n_col, cap, 2 * tile_cols)
        got = lax.all_to_all(sent, ("row", "col"), split_axis=0, concat_axis=0, tiled=True)
        tile = jnp.dot(placer, got.reshape(-1, 2 * tile_cols), preferred_element_type=F32)
        tiles.append(tile.astype(BF16))

    rights = []
    for f in range(FREQ):
        rights.append([])
        for j in range(THIRDS):
            real = tiles[f][:, j * sub : (j + 1) * sub]
            imag = tiles[f][:, tile_cols + j * sub : tile_cols + (j + 1) * sub]
            rights[f].append(
                lax.all_gather(jnp.concatenate([real, imag], axis=1), "row", axis=0, tiled=True)
            )

    keys = list(range(n_col))
    tile_offs = jnp.stack([(me ^ d) * tile_cols for d in keys])
    sub_offs = jnp.stack([(me ^ d) * tile_cols + j * sub for j in range(THIRDS) for d in keys])
    outs = [[], []]
    for f in range(FREQ):
        held = gather_cols(tiles[f], n_col)
        lefts = [held[d] for d in keys]
        first = []
        gathered = []
        for j in range(THIRDS):
            piece = complex_product(tile_offs, lefts, rights[f][j], weight)
            first.append(piece)
            held = gather_cols(piece, n_col)
            gathered += [held[d] for d in keys]
        second = [complex_product(sub_offs, gathered, rights[f][j], weight) for j in range(THIRDS)]
        for k, pieces in enumerate((first, second)):
            outs[k].append(jnp.concatenate([p[:, :sub] for p in pieces], axis=1))
            outs[k].append(jnp.concatenate([p[:, sub:] for p in pieces], axis=1))
    return jnp.stack([jnp.stack(o, axis=0) for o in outs], axis=0)


def solution(mesh):
    placed = (
        P(("groups", "row", "col"), None, None),
        P(("groups", "row", "col")),
        P(("groups", "row", "col")),
    )
    return jax.shard_map(
        per_device,
        mesh=mesh,
        in_specs=placed,
        out_specs=P("groups", None, "row", "col"),
        check_vma=False,
    )
```

```python
import functools
import math

import jax
import jax.numpy as jnp
from jax import lax
from jax.experimental import pallas as pl
from jax.experimental.pallas import tpu as pltpu
from jax.sharding import PartitionSpec as P

NS = 3072
FREQ = 2
THIRDS = 3
BF16 = jnp.bfloat16
F32 = jnp.float32


def after(value, earlier):
    return lax.optimization_barrier((value, earlier))[0]


def gather_cols(piece, n_col):
    held = {0: piece}
    bit = n_col // 2
    while bit:
        pairs = [(c, c ^ bit) for c in range(n_col)]
        arrived = {d ^ bit: lax.ppermute(a, "col", pairs) for d, a in held.items()}
        held.update(arrived)
        bit //= 2
    return [held[d] for d in range(n_col)]


def hop(pair, k, n_row):
    down = [(r, r - 1) for r in range(1, n_row) if r + k - 1 < n_row]
    up = [(r, r + 1) for r in range(n_row - 1) if r - k + 1 >= 0]
    return lax.ppermute(pair[0], "row", down), lax.ppermute(pair[1], "row", up)


def bin_kernel(picker, data, out0, out1):
    hits = picker[...]
    n_row, cap = out0.shape[0], out0.shape[2]
    sub = data.shape[2] // THIRDS
    for p in range(2 * FREQ):
        out = out0 if p < 2 else out1
        rows = jnp.dot(hits, data[p], preferred_element_type=F32).astype(BF16)
        for b in range(n_row):
            for j in range(THIRDS):
                start = (2 * j + p % 2) * sub
                out[b, 0, :, start : start + sub] = rows[b * cap : (b + 1) * cap, j * sub : (j + 1) * sub]


def bin_rows(picker, data, n_row, n_col):
    planes, own_cap, order = data.shape
    cap = picker.shape[0] // n_row
    wide = 2 * order // n_col
    shape = jax.ShapeDtypeStruct((n_row, n_col, cap, wide), BF16)
    block = pl.BlockSpec((n_row, 1, cap, wide), lambda c: (0, c, 0, 0))
    return pl.pallas_call(
        bin_kernel,
        grid=(n_col,),
        in_specs=[
            pl.BlockSpec(picker.shape, lambda c: (0, 0)),
            pl.BlockSpec((planes, own_cap, order // n_col), lambda c: (0, 0, c)),
        ],
        out_specs=[block, block],
        out_shape=[shape, shape],
        compiler_params=pltpu.CompilerParams(vmem_limit_bytes=40 * 2**20),
        cost_estimate=pl.CostEstimate(
            flops=2 * picker.shape[0] * own_cap * planes * order,
            bytes_accessed=4 * planes * own_cap * order,
            transcendentals=0,
        ),
    )(picker, data)


def product_kernel(plan, n_left, has_piece, weight, spots, *refs):
    lefts, refs = refs[:n_left], refs[n_left:]
    sources, refs = refs[: len(plan)], refs[len(plan) :]
    *outs, right, sems = refs[-(4 if has_piece else 3) :]
    whole, piece = outs[0], (outs[1] if has_piece else None)
    rows_at = spots[n_left]
    block = sources[0].shape[0]

    @pl.when(pl.program_id(0) == 0)
    def _():
        for phase in range(2):
            for s, (low, high, step) in enumerate(plan):

                @pl.when((rows_at >= low) & (rows_at <= high))
                def _(s=s, step=step):
                    start = pl.multiple_of((rows_at + step) * block if len(plan) > 1 else 0, 32)
                    copy = pltpu.make_async_copy(sources[s], right.at[pl.ds(start, block)], sems.at[s])
                    if phase == 0:
                        copy.start()
                    else:
                        copy.wait()

    width = right.shape[1] // 2
    tile = lefts[0].shape[0]
    by_real = jnp.zeros((tile, 2 * width), F32)
    by_imag = jnp.zeros((tile, 2 * width), F32)
    for i, left in enumerate(lefts):
        depth = left.shape[1] // 2
        part = right[pl.ds(pl.multiple_of(spots[i], 128), depth), :]
        by_real += jnp.dot(left[:, :depth], part, preferred_element_type=F32)
        by_imag += jnp.dot(left[:, depth:], part, preferred_element_type=F32)
    real = ((by_real[:, :width] - by_imag[:, width:]) * weight).astype(BF16)
    imag = ((by_real[:, width:] + by_imag[:, :width]) * weight).astype(BF16)
    whole[0, 0] = real
    whole[0, 1] = imag
    if has_piece:
        piece[:, :width] = real
        piece[:, width:] = imag


def complex_product(spots, lefts, sources, plan, result, at, shape, weight):
    n, f, j = at
    has_piece = n == 0
    rows = lefts[0].shape[0]
    tile = 256 if rows % 256 == 0 else rows
    wide = sources[0].shape[1]
    held = [] if result is None else [result]
    out_specs = [pl.BlockSpec((1, 2, tile, wide // 2), lambda i, s: (n, f, i, j))]
    out_shape = [jax.ShapeDtypeStruct(shape, BF16)]
    if has_piece:
        out_specs.append(pl.BlockSpec((tile, wide), lambda i, s: (i, 0)))
        out_shape.append(jax.ShapeDtypeStruct((rows, wide), BF16))
    spec = pltpu.PrefetchScalarGridSpec(
        num_scalar_prefetch=1,
        grid=(rows // tile,),
        in_specs=[pl.BlockSpec((tile, a.shape[1]), lambda i, s: (i, 0)) for a in lefts]
        + [pl.BlockSpec(memory_space=pl.ANY)] * (len(sources) + len(held)),
        out_specs=out_specs,
        scratch_shapes=[pltpu.VMEM((NS, wide), BF16), pltpu.SemaphoreType.DMA((len(plan),))],
    )
    return pl.pallas_call(
        functools.partial(product_kernel, plan, len(lefts), has_piece, weight),
        grid_spec=spec,
        out_shape=out_shape,
        input_output_aliases={1 + len(lefts) + len(sources): 0} if held else {},
        compiler_params=pltpu.CompilerParams(vmem_limit_bytes=40 * 2**20),
        cost_estimate=pl.CostEstimate(
            flops=4 * rows * NS * wide, bytes_accessed=2 * NS * (wide + 2 * rows), transcendentals=0
        ),
    )(spots, *lefts, *sources, *held)


def per_device(acq_data, grid_row, counts):
    n_row = lax.axis_size("row")
    n_col = lax.axis_size("col")
    own_cap, planes, order = acq_data.shape
    block_rows = order // n_row
    tile_cols = order // n_col
    cap = own_cap // n_row
    slots = n_row * cap
    sub = tile_cols // THIRDS
    weight = 1.0 / math.sqrt(2.0 * NS)
    me = lax.axis_index("col")

    slot_index = jnp.arange(own_cap, dtype=jnp.int32)
    block = jnp.where(slot_index < counts[0], grid_row // block_rows, n_row)
    earlier = (block[None, :] == block[:, None]) & (slot_index[None, :] < slot_index[:, None])
    rank = jnp.sum(earlier.astype(jnp.int32), axis=1)
    leaving = jnp.where(block < n_row, block * cap + rank, -1)
    hit = jnp.arange(slots, dtype=jnp.int32)[:, None] == leaving[None, :]
    spots = jnp.sum(jnp.where(hit, (grid_row % block_rows)[None, :] + 1, 0), axis=1) - 1
    labels = jnp.broadcast_to(spots.reshape(n_row, 1, cap), (n_row, n_col, cap))
    places = lax.all_to_all(
        labels.reshape(n_row * n_col, cap), ("row", "col"), split_axis=0, concat_axis=0, tiled=True
    ).reshape(-1)
    placer = (jnp.arange(block_rows, dtype=jnp.int32)[:, None] == places[None, :]).astype(BF16)
    sent = bin_rows(hit.astype(BF16), jnp.transpose(acq_data, (1, 0, 2)), n_row, n_col)

    tiles = []
    for f in range(FREQ):
        got = lax.all_to_all(
            sent[f].reshape(n_row * n_col, cap, 2 * tile_cols),
            ("row", "col"),
            split_axis=0,
            concat_axis=0,
            tiled=True,
        ).reshape(-1, 2 * tile_cols)
        tiles.append(
            [
                jnp.dot(placer, got[:, 2 * j * sub : 2 * (j + 1) * sub], preferred_element_type=F32).astype(BF16)
                for j in range(THIRDS)
            ]
        )

    if n_row <= 4:
        plan = [(0, n_row - 1, 0)]
        for k in range(1, n_row):
            plan += [(0, n_row - 1 - k, k), (k, n_row - 1, -k)]
        rights = []
        passed = None
        for f in range(FREQ):
            begun = tiles[f] if passed is None else [after(t, p) for t, p in zip(tiles[f], passed)]
            carried = [(t, t) for t in begun]
            found = [[t] for t in tiles[f]]
            for k in range(1, n_row):
                carried = [hop(pair, k, n_row) for pair in carried]
                for j in range(THIRDS):
                    found[j] += list(carried[j])
                if k == n_row - 2:
                    passed = carried
            rights.append(found)
    else:
        plan = [(0, n_row - 1, 0)]
        rights = [[[lax.all_gather(t, "row", axis=0, tiled=True)] for t in tiles[f]] for f in range(FREQ)]

    spots = jnp.stack(
        [(me ^ d) * tile_cols + j * sub for j in range(THIRDS) for d in range(n_col)] + [lax.axis_index("row")]
    ).astype(jnp.int32)
    shape = (2, planes, block_rows, tile_cols)
    result = None
    for f in range(FREQ):
        lefts = []
        for j in range(THIRDS):
            lefts += gather_cols(tiles[f][j], n_col)
        gathered = []
        for j in range(THIRDS):
            result, piece = complex_product(spots, lefts, rights[f][j], plan, result, (0, f, j), shape, weight)
            gathered += gather_cols(piece, n_col)
        for j in range(THIRDS):
            (result,) = complex_product(spots, gathered, rights[f][j], plan, result, (1, f, j), shape, weight)
    return result


def solution(mesh):
    placed = (
        P(("groups", "row", "col"), None, None),
        P(("groups", "row", "col")),
        P(("groups", "row", "col")),
    )
    return jax.shard_map(
        per_device,
        mesh=mesh,
        in_specs=placed,
        out_specs=P("groups", None, "row", "col"),
        check_vma=False,
    )
```

```python
import functools
import math

import jax
import jax.numpy as jnp
from jax import lax
from jax.experimental import pallas as pl
from jax.experimental.pallas import tpu as pltpu
from jax.sharding import PartitionSpec as P

NS = 3072
FREQ = 2
THIRDS = 3
BF16 = jnp.bfloat16
F32 = jnp.float32


def hop(pair, k, n_row):
    down = [(r, r - 1) for r in range(1, n_row) if r + k - 1 < n_row]
    up = [(r, r + 1) for r in range(n_row - 1) if r - k + 1 >= 0]
    return lax.ppermute(pair[0], "row", down), lax.ppermute(pair[1], "row", up)


def bin_kernel(picker, data, out):
    n_row, cap = out.shape[0], out.shape[2]
    sub = data.shape[2]
    for p in range(2):
        rows = jnp.dot(picker[...], data[p], preferred_element_type=F32).astype(BF16)
        for b in range(n_row):
            out[b, 0, :, p * sub : (p + 1) * sub] = rows[b * cap : (b + 1) * cap]


def bin_rows(picker, data, f, thirds, n_row, n_col):
    planes, own_cap, order = data.shape
    cap = picker.shape[0] // n_row
    sub = order // n_col // THIRDS
    count, first = len(thirds), thirds[0]
    return pl.pallas_call(
        bin_kernel,
        grid=(n_col, count),
        in_specs=[
            pl.BlockSpec(picker.shape, lambda c, j: (0, 0)),
            pl.BlockSpec((2, own_cap, sub), lambda c, j: (f, 0, c * THIRDS + first + j)),
        ],
        out_specs=pl.BlockSpec((n_row, 1, cap, 2 * sub), lambda c, j: (0, c, 0, j)),
        out_shape=jax.ShapeDtypeStruct((n_row, n_col, cap, 2 * sub * count), BF16),
        compiler_params=pltpu.CompilerParams(vmem_limit_bytes=16 * 2**20),
        cost_estimate=pl.CostEstimate(
            flops=4 * picker.shape[0] * own_cap * n_col * count * sub,
            bytes_accessed=8 * own_cap * n_col * count * sub,
            transcendentals=0,
        ),
    )(picker, data)


def product_kernel(opts, at_row, *refs):
    plan, thirds, order, weight = opts["plan"], opts["thirds"], opts["order"], opts["weight"]
    lefts, refs = refs[: len(thirds)], refs[len(thirds) :]
    sources, refs = refs[: len(plan)], refs[len(plan) :]
    before = refs[0] if opts["before"] else None
    *outs, right, sems = refs[opts["before"] + opts["held"] :]
    row = at_row[0]
    block = sources[0].shape[0]

    @pl.when(pl.program_id(0) == 0)
    def _():
        for phase in range(2):
            for s, (low, high, step) in enumerate(plan):

                @pl.when((row >= low) & (row <= high))
                def _(s=s, step=step):
                    start = pl.multiple_of((row + step) * block if len(plan) > 1 else 0, 32)
                    copy = pltpu.make_async_copy(sources[s], right.at[pl.ds(start, block)], sems.at[s])
                    if phase == 0:
                        copy.start()
                    else:
                        copy.wait()

    sub = right.shape[1] // 2
    real_left, imag_left, parts = [], [], []
    for c in range(lefts[0].shape[0]):
        for left, group in zip(lefts, thirds):
            for k, j in enumerate(group):
                real_left.append(left[c, :, 2 * k * sub : (2 * k + 1) * sub])
                imag_left.append(left[c, :, (2 * k + 1) * sub : (2 * k + 2) * sub])
                parts.append((c * THIRDS + j) * sub)
    if len(parts) * sub == NS and parts == sorted(parts):
        rows = right[...]
    else:
        rows = jnp.concatenate([right[p : p + sub] for p in parts], axis=0)
    by_real = jnp.dot(jnp.concatenate(real_left, axis=1), rows, preferred_element_type=F32)
    by_imag = jnp.dot(jnp.concatenate(imag_left, axis=1), rows, preferred_element_type=F32)
    real = by_real[:, :sub] - by_imag[:, sub:]
    imag = by_real[:, sub:] + by_imag[:, :sub]
    if before is not None:
        real = real + before[:, :sub]
        imag = imag + before[:, sub:]
    if order is None:
        outs[0][:, :sub] = real
        outs[0][:, sub:] = imag
        return
    real = (real * weight).astype(BF16)
    imag = (imag * weight).astype(BF16)
    outs[0][0, 0] = real
    outs[0][0, 1] = imag
    if len(outs) > 1:
        outs[1][:, :sub] = real
        outs[1][:, sub:] = imag


def complex_product(row, lefts, right, shape, held, at, before=None, piece_at=(0, 1)):
    plan, sources = right
    thirds = [group for _, group in lefts]
    lefts = [a for a, _ in lefts]
    n_col, rows, _ = lefts[0].shape
    tile = 256 if rows % 256 == 0 else rows
    wide = sources[0].shape[1]
    sub = wide // 2
    order = None
    if at is None:
        out_specs = [pl.BlockSpec((tile, wide), lambda i, s: (i, 0))]
        out_shape = [jax.ShapeDtypeStruct((rows, wide), F32)]
    else:
        order, f, j = at
        out_specs = [pl.BlockSpec((1, 2, tile, sub), lambda i, s: (order, f, i, j))]
        out_shape = [jax.ShapeDtypeStruct(shape, BF16)]
        if order == 0:
            which, of = piece_at
            out_specs.append(pl.BlockSpec((tile, wide), lambda i, s: (i, which)))
            out_shape.append(jax.ShapeDtypeStruct((rows, of * wide), BF16))
    in_specs = [pl.BlockSpec((n_col, tile, a.shape[2]), lambda i, s: (0, i, 0)) for a in lefts]
    in_specs += [pl.BlockSpec(memory_space=pl.ANY)] * len(sources)
    args = [*lefts, *sources]
    if before is not None:
        in_specs.append(pl.BlockSpec((tile, wide), lambda i, s: (i, 0)))
        args.append(before)
    aliases = {1 + len(args) + k: k for k in range(len(held))}
    in_specs += [pl.BlockSpec(memory_space=pl.ANY)] * len(held)
    depth = sum(len(g) for g in thirds) * n_col * sub
    opts = dict(
        plan=plan,
        thirds=thirds,
        order=order,
        weight=1.0 / math.sqrt(2.0 * NS),
        before=int(before is not None),
        held=len(held),
    )
    return pl.pallas_call(
        functools.partial(product_kernel, opts),
        grid_spec=pltpu.PrefetchScalarGridSpec(
            num_scalar_prefetch=1,
            grid=(rows // tile,),
            in_specs=in_specs,
            out_specs=out_specs,
            scratch_shapes=[pltpu.VMEM((NS, wide), BF16), pltpu.SemaphoreType.DMA((len(plan),))],
        ),
        out_shape=out_shape,
        input_output_aliases=aliases,
        compiler_params=pltpu.CompilerParams(vmem_limit_bytes=48 * 2**20),
        cost_estimate=pl.CostEstimate(
            flops=4 * rows * depth * wide, bytes_accessed=2 * NS * wide + 4 * rows * depth, transcendentals=0
        ),
    )(row, *args, *held)


def per_device(acq_data, grid_row, counts):
    n_row = lax.axis_size("row")
    n_col = lax.axis_size("col")
    own_cap, planes, order = acq_data.shape
    block_rows = order // n_row
    tile_cols = order // n_col
    cap = own_cap // n_row
    slots = n_row * cap
    wide = 2 * tile_cols // THIRDS
    everything = tuple(range(THIRDS))

    slot_index = jnp.arange(own_cap, dtype=jnp.int32)
    block = jnp.where(slot_index < counts[0], grid_row // block_rows, n_row)
    earlier = (block[None, :] == block[:, None]) & (slot_index[None, :] < slot_index[:, None])
    rank = jnp.sum(earlier.astype(jnp.int32), axis=1)
    leaving = jnp.where(block < n_row, block * cap + rank, -1)
    hit = jnp.arange(slots, dtype=jnp.int32)[:, None] == leaving[None, :]
    spots = jnp.sum(jnp.where(hit, (grid_row % block_rows)[None, :] + 1, 0), axis=1) - 1
    labels = jnp.broadcast_to(spots.reshape(n_row, 1, cap), (n_row, n_col, cap))
    places = lax.all_to_all(
        labels.reshape(n_row * n_col, cap), ("row", "col"), split_axis=0, concat_axis=0, tiled=True
    ).reshape(-1)
    picker = hit.astype(BF16)
    placer = (jnp.arange(block_rows, dtype=jnp.int32)[:, None] == places[None, :]).astype(BF16)
    data = jnp.transpose(acq_data, (1, 0, 2))

    tiles = {}
    lefts = [[], []]
    for f, group in ((0, (0,)), (0, (1, 2)), (1, everything)):
        sent = bin_rows(picker, data, f, group, n_row, n_col)
        got = lax.all_to_all(
            sent.reshape(n_row * n_col, cap, wide * len(group)), ("row", "col"), split_axis=0, concat_axis=0, tiled=True
        ).reshape(-1, wide * len(group))
        tile = jnp.dot(placer, got, preferred_element_type=F32).astype(BF16)
        lefts[f].append((lax.all_gather(tile, "col", axis=0), group))
        for k, j in enumerate(group):
            tiles[f, j] = tile[:, k * wide : (k + 1) * wide]

    rights = {}
    plan = [(0, n_row - 1, 0)]
    if n_row <= 4:
        for k in range(1, n_row):
            plan += [(0, n_row - 1 - k, k), (k, n_row - 1, -k)]
        for key, tile in tiles.items():
            found = [tile]
            pair = (tile, tile)
            for k in range(1, n_row):
                pair = hop(pair, k, n_row)
                found += list(pair)
            rights[key] = (plan, found)
    else:
        for key, tile in tiles.items():
            rights[key] = (plan, [lax.all_gather(tile, "row", axis=0, tiled=True)])

    row = lax.axis_index("row").astype(jnp.int32).reshape(1)
    shape = (2, planes, block_rows, tile_cols)
    result = ()
    piece = ()
    for j in everything:
        result, piece = complex_product(row, lefts[0], rights[0, j], shape, (*result, *piece), (0, 0, j), piece_at=(j, 3))
        result, piece = (result,), (piece,)
    gathered = [(lax.all_gather(piece[0], "col", axis=0), everything)]
    for j in everything:
        result = complex_product(row, gathered, rights[0, j], shape, result, (1, 0, j))
    gathered = []
    for j in everything:
        *result, piece = complex_product(row, lefts[1], rights[1, j], shape, result, (0, 1, j))
        gathered.append((lax.all_gather(piece, "col", axis=0), (j,)))
    sums = []
    for j in everything:
        sums += complex_product(row, gathered[:2], rights[1, j], shape, (), None)
    for j in everything:
        result = complex_product(row, gathered[2:], rights[1, j], shape, result, (1, 1, j), before=sums[j])
    return result[0]


def solution(mesh):
    placed = (
        P(("groups", "row", "col"), None, None),
        P(("groups", "row", "col")),
        P(("groups", "row", "col")),
    )
    return jax.shard_map(
        per_device,
        mesh=mesh,
        in_specs=placed,
        out_specs=P("groups", None, "row", "col"),
        check_vma=False,
    )
```

```python
import functools
import math

import jax
import jax.numpy as jnp
from jax import lax
from jax.experimental import pallas as pl
from jax.experimental.pallas import tpu as pltpu
from jax.sharding import PartitionSpec as P

NS = 3072
FREQ = 2
THIRDS = 3
BF16 = jnp.bfloat16
F32 = jnp.float32


def hop(pair, k, n_row):
    down = [(r, r - 1) for r in range(1, n_row) if r + k - 1 < n_row]
    up = [(r, r + 1) for r in range(n_row - 1) if r - k + 1 >= 0]
    return lax.ppermute(pair[0], "row", down), lax.ppermute(pair[1], "row", up)


def bin_kernel(picker, data, out):
    n_row, cap = out.shape[0], out.shape[2]
    sub = data.shape[2]
    for p in range(2):
        rows = jnp.dot(picker[...], data[p], preferred_element_type=F32).astype(BF16)
        for b in range(n_row):
            out[b, 0, :, p * sub : (p + 1) * sub] = rows[b * cap : (b + 1) * cap]


def bin_rows(picker, data, f, thirds, n_row, n_col):
    planes, own_cap, order = data.shape
    cap = picker.shape[0] // n_row
    sub = order // n_col // THIRDS
    count, first = len(thirds), thirds[0]
    return pl.pallas_call(
        bin_kernel,
        grid=(n_col, count),
        in_specs=[
            pl.BlockSpec(picker.shape, lambda c, j: (0, 0)),
            pl.BlockSpec((2, own_cap, sub), lambda c, j: (f, 0, c * THIRDS + first + j)),
        ],
        out_specs=pl.BlockSpec((n_row, 1, cap, 2 * sub), lambda c, j: (0, c, 0, j)),
        out_shape=jax.ShapeDtypeStruct((n_row, n_col, cap, 2 * sub * count), BF16),
        compiler_params=pltpu.CompilerParams(vmem_limit_bytes=16 * 2**20),
        cost_estimate=pl.CostEstimate(
            flops=4 * picker.shape[0] * own_cap * n_col * count * sub,
            bytes_accessed=8 * own_cap * n_col * count * sub,
            transcendentals=0,
        ),
    )(picker, data)


def after(value, earlier):
    return lax.optimization_barrier((value, earlier))[0]


def gather_cols(piece, n_col):
    held = {0: piece}
    bit = n_col // 2
    while bit:
        pairs = [(c, c ^ bit) for c in range(n_col)]
        arrived = {d ^ bit: lax.ppermute(a, "col", pairs) for d, a in held.items()}
        held.update(arrived)
        bit //= 2
    return [held[d] for d in range(n_col)]


def product_kernel(opts, where, *refs):
    plan, groups, order, n_col = opts["plan"], opts["groups"], opts["order"], opts["n_col"]
    lefts, refs = refs[: opts["lefts"]], refs[opts["lefts"] :]
    sources, refs = refs[: opts["outs"] * len(plan)], refs[opts["outs"] * len(plan) :]
    before = refs[0] if opts["before"] else None
    *outs, right, sems = refs[opts["before"] + opts["held"] :]
    row, me = where[0], where[1]
    sub = right.shape[2] // 2
    depth = right.shape[1] // n_col
    first = groups[0][0] * sub
    third = pl.program_id(1)

    def copies(t, phase):
        for s, (low, high, step) in enumerate(plan):
            source = sources[t * len(plan) + s]
            if len(plan) == 1:
                for c in range(n_col):
                    copy = pltpu.make_async_copy(
                        source.at[pl.ds(c * sub * THIRDS + first, depth)],
                        right.at[t, pl.ds(c * depth, depth)],
                        sems.at[t, c],
                    )
                    copy.start() if phase == 0 else copy.wait()
                continue

            @pl.when((row >= low) & (row <= high))
            def _(s=s, step=step, source=source):
                start = pl.multiple_of((row + step) * depth, 32)
                copy = pltpu.make_async_copy(
                    source.at[pl.ds(first, depth)], right.at[t, pl.ds(start, depth)], sems.at[t, s]
                )
                copy.start() if phase == 0 else copy.wait()

    for t in range(opts["outs"]):

        @pl.when((pl.program_id(0) == 0) & (third == 0))
        def _(t=t):
            copies(t, 0)

    for t in range(opts["outs"]):

        @pl.when((pl.program_id(0) == 0) & (third == t))
        def _(t=t):
            copies(t, 1)

    tile = lefts[0].shape[-2]
    by_real = jnp.zeros((tile, 2 * sub), F32)
    by_imag = jnp.zeros((tile, 2 * sub), F32)
    for c in range(n_col):
        if opts["by_xor"]:
            real_left, imag_left = [lefts[c][:, :sub]], [lefts[c][:, sub:]]
            start = pl.multiple_of((me ^ c) * depth, 32)
        else:
            real_left, imag_left = [], []
            start = c * depth
            for left, group in zip(lefts, groups):
                for k in range(len(group)):
                    real_left.append(left[c, :, 2 * k * sub : (2 * k + 1) * sub])
                    imag_left.append(left[c, :, (2 * k + 1) * sub : (2 * k + 2) * sub])
        rows = right[third, pl.ds(start, depth), :]
        by_real += jnp.dot(jnp.concatenate(real_left, axis=1), rows, preferred_element_type=F32)
        by_imag += jnp.dot(jnp.concatenate(imag_left, axis=1), rows, preferred_element_type=F32)
    real = by_real[:, :sub] - by_imag[:, sub:]
    imag = by_real[:, sub:] + by_imag[:, :sub]
    if before is not None:
        real = real + before[:, :sub]
        imag = imag + before[:, sub:]
    if order is None:
        outs[0][:, :sub] = real
        outs[0][:, sub:] = imag
        return
    real = (real * opts["weight"]).astype(BF16)
    imag = (imag * opts["weight"]).astype(BF16)
    outs[0][0, 0] = real
    outs[0][0, 1] = imag
    if len(outs) > 1:
        outs[1][:, :sub] = real
        outs[1][:, sub:] = imag


def complex_product(where, lefts, plan, rights, shape, held, at, before=None, piece_at=(0, 1)):
    groups = [group for _, group in lefts]
    by_xor = isinstance(lefts[0][0], list)
    arrays = lefts[0][0] if by_xor else [a for a, _ in lefts]
    n_col = len(arrays) if by_xor else arrays[0].shape[0]
    rows = arrays[0].shape[-2]
    tile = 256 if rows % 256 == 0 else rows
    wide = rights[0][0].shape[1]
    sub = wide // 2
    count = len(rights)
    order = None
    if at is None:
        out_specs = [pl.BlockSpec((tile, wide), lambda i, j, s: (i, j))]
        out_shape = [jax.ShapeDtypeStruct((rows, count * wide), F32)]
    else:
        order, f, first = at
        out_specs = [pl.BlockSpec((1, 2, tile, sub), lambda i, j, s: (order, f, i, first + j))]
        out_shape = [jax.ShapeDtypeStruct(shape, BF16)]
        if order == 0:
            which, of = piece_at
            out_specs.append(pl.BlockSpec((tile, wide), lambda i, j, s: (i, which + j)))
            out_shape.append(jax.ShapeDtypeStruct((rows, of * wide), BF16))
    if by_xor:
        in_specs = [pl.BlockSpec((tile, wide), lambda i, j, s: (i, 0)) for a in arrays]
    else:
        in_specs = [pl.BlockSpec((n_col, tile, a.shape[2]), lambda i, j, s: (0, i, 0)) for a in arrays]
    sources = [a for found in rights for a in found]
    in_specs += [pl.BlockSpec(memory_space=pl.ANY)] * len(sources)
    args = [*arrays, *sources]
    if before is not None:
        in_specs.append(pl.BlockSpec((tile, wide), lambda i, j, s: (i, j)))
        args.append(before)
    aliases = {1 + len(args) + k: k for k in range(len(held))}
    in_specs += [pl.BlockSpec(memory_space=pl.ANY)] * len(held)
    depth = sum(len(g) for g in groups) * n_col * sub
    opts = dict(
        plan=plan,
        groups=groups,
        order=order,
        n_col=n_col,
        lefts=len(arrays),
        outs=count,
        by_xor=by_xor,
        weight=1.0 / math.sqrt(2.0 * NS),
        before=int(before is not None),
        held=len(held),
    )
    return pl.pallas_call(
        functools.partial(product_kernel, opts),
        grid_spec=pltpu.PrefetchScalarGridSpec(
            num_scalar_prefetch=1,
            grid=(rows // tile, count),
            in_specs=in_specs,
            out_specs=out_specs,
            scratch_shapes=[
                pltpu.VMEM((count, depth, wide), BF16),
                pltpu.SemaphoreType.DMA((count, max(len(plan), n_col))),
            ],
        ),
        out_shape=out_shape,
        input_output_aliases=aliases,
        compiler_params=pltpu.CompilerParams(vmem_limit_bytes=48 * 2**20),
        cost_estimate=pl.CostEstimate(
            flops=4 * rows * depth * wide * count,
            bytes_accessed=2 * depth * wide * count + 4 * rows * depth,
            transcendentals=0,
        ),
    )(where, *args, *held)


def per_device(acq_data, grid_row, counts):
    n_row = lax.axis_size("row")
    n_col = lax.axis_size("col")
    own_cap, planes, order = acq_data.shape
    block_rows = order // n_row
    tile_cols = order // n_col
    cap = own_cap // n_row
    slots = n_row * cap
    wide = 2 * tile_cols // THIRDS
    everything = tuple(range(THIRDS))

    slot_index = jnp.arange(own_cap, dtype=jnp.int32)
    block = jnp.where(slot_index < counts[0], grid_row // block_rows, n_row)
    earlier = (block[None, :] == block[:, None]) & (slot_index[None, :] < slot_index[:, None])
    rank = jnp.sum(earlier.astype(jnp.int32), axis=1)
    leaving = jnp.where(block < n_row, block * cap + rank, -1)
    hit = jnp.arange(slots, dtype=jnp.int32)[:, None] == leaving[None, :]
    spots = jnp.sum(jnp.where(hit, (grid_row % block_rows)[None, :] + 1, 0), axis=1) - 1
    picker = hit.astype(BF16)
    data = jnp.transpose(acq_data, (1, 0, 2))
    line = n_row <= 4 and block_rows == tile_cols
    plan = [(0, n_row - 1, 0)]
    if line:
        for k in range(1, n_row):
            plan += [(0, n_row - 1 - k, k), (k, n_row - 1, -k)]

    keys = [(f, j) for f in range(FREQ) for j in everything]
    sent = bin_rows(picker, data, 0, (0,), n_row, n_col)
    labels = jnp.broadcast_to(after(spots, sent).reshape(n_row, 1, cap), (n_row, n_col, cap))
    places = lax.all_to_all(
        labels.reshape(n_row * n_col, cap), ("row", "col"), split_axis=0, concat_axis=0, tiled=True
    ).reshape(-1)
    placer = (jnp.arange(block_rows, dtype=jnp.int32)[:, None] == places[None, :]).astype(BF16)

    pieces, pairs, rights = [], {}, {key: [] for key in keys}
    lefts = [[], []]
    for p, (f, j) in enumerate(keys):
        if p:
            sent = bin_rows(picker, data, f, (j,), n_row, n_col)
        if line and p >= 2:
            sent = after(sent, pairs[p - 2, 1])
        got = lax.all_to_all(
            sent.reshape(n_row * n_col, cap, wide), ("row", "col"), split_axis=0, concat_axis=0, tiled=True
        ).reshape(-1, wide)
        tile = jnp.dot(placer, got, preferred_element_type=F32).astype(BF16)
        lefts[f].append((lax.all_gather(tile, "col", axis=0), (j,)))
        pieces.append(tile)
        if not line:
            rights[f, j] = [lax.all_gather(tile, "row", axis=0, tiled=True)]
            continue
        pairs[p, 1] = hop((tile, tile), 1, n_row)
        if p >= 2:
            for k in range(2, n_row):
                begun = pairs[p - 2, k - 1]
                pairs[p - 2, k] = hop(after(begun, got) if k == n_row - 1 else begun, k, n_row)
    if line:
        last = len(keys) - 1
        for k in range(2, n_row):
            pairs[last - 1, k] = hop(after(pairs[last - 1, k - 1], pairs[last, k - 1]), k, n_row)
            pairs[last, k] = hop(pairs[last, k - 1], k, n_row)
        for p, key in enumerate(keys):
            rights[key] = [pieces[p]] + [a for k in range(1, n_row) for a in pairs[p, k]]

    where = jnp.stack([lax.axis_index("row"), lax.axis_index("col")]).astype(jnp.int32)
    product = functools.partial(complex_product, where)
    shape = (2, planes, block_rows, tile_cols)
    held = ()
    for j in everything:
        held = product(lefts[0], plan, [rights[0, j]], shape, tuple(held), (0, 0, j), piece_at=(j, THIRDS))
    result, piece = held
    gathered = [(lax.all_gather(piece, "col", axis=0), everything)]
    for j in everything:
        (result,) = product(gathered, plan, [rights[0, j]], shape, (result,), (1, 0, j))
    gathered = []
    for j in everything:
        result, piece = product(lefts[1], plan, [rights[1, j]], shape, (result,), (0, 1, j))
        gathered.append((gather_cols(piece, n_col) if j == THIRDS - 1 else lax.all_gather(piece, "col", axis=0), (j,)))
    final = [rights[1, j] for j in everything]
    (sums,) = product(gathered[:-1], plan, final, shape, (), None)
    return product(gathered[-1:], plan, final, shape, (result,), (1, 1, 0), before=sums)[0]


def solution(mesh):
    placed = (
        P(("groups", "row", "col"), None, None),
        P(("groups", "row", "col")),
        P(("groups", "row", "col")),
    )
    return jax.shard_map(
        per_device,
        mesh=mesh,
        in_specs=placed,
        out_specs=P("groups", None, "row", "col"),
        check_vma=False,
    )
```

```python
import functools
import math

import jax
import jax.numpy as jnp
from jax import lax
from jax.experimental import pallas as pl
from jax.experimental.pallas import tpu as pltpu
from jax.sharding import PartitionSpec as P

NS = 3072
FREQ = 2
THIRDS = 3
BF16 = jnp.bfloat16
F32 = jnp.float32


def hop(pair, k, n_row):
    down = [(r, r - 1) for r in range(1, n_row) if r + k - 1 < n_row]
    up = [(r, r + 1) for r in range(n_row - 1) if r - k + 1 >= 0]
    return lax.ppermute(pair[0], "row", down), lax.ppermute(pair[1], "row", up)


def bin_kernel(picker, data, out):
    n_row, cap = out.shape[0], out.shape[2]
    sub = data.shape[2]
    for p in range(2):
        rows = jnp.dot(picker[...], data[p], preferred_element_type=F32).astype(BF16)
        for b in range(n_row):
            out[b, 0, :, p * sub : (p + 1) * sub] = rows[b * cap : (b + 1) * cap]


def bin_rows(picker, data, f, thirds, n_row, n_col):
    planes, own_cap, order = data.shape
    cap = picker.shape[0] // n_row
    sub = order // n_col // THIRDS
    count, first = len(thirds), thirds[0]
    return pl.pallas_call(
        bin_kernel,
        grid=(n_col, count),
        in_specs=[
            pl.BlockSpec(picker.shape, lambda c, j: (0, 0)),
            pl.BlockSpec((2, own_cap, sub), lambda c, j: (f, 0, c * THIRDS + first + j)),
        ],
        out_specs=pl.BlockSpec((n_row, 1, cap, 2 * sub), lambda c, j: (0, c, 0, j)),
        out_shape=jax.ShapeDtypeStruct((n_row, n_col, cap, 2 * sub * count), BF16),
        compiler_params=pltpu.CompilerParams(vmem_limit_bytes=16 * 2**20),
        cost_estimate=pl.CostEstimate(flops=1000, bytes_accessed=1000, transcendentals=0),
    )(picker, data)


def after(value, earlier):
    return lax.optimization_barrier((value, earlier))[0]


def gather_cols(piece, n_col):
    held = {0: piece}
    bit = n_col // 2
    while bit:
        pairs = [(c, c ^ bit) for c in range(n_col)]
        arrived = {d ^ bit: lax.ppermute(a, "col", pairs) for d, a in held.items()}
        held.update(arrived)
        bit //= 2
    return [held[d] for d in range(n_col)]


def product_kernel(opts, where, *refs):
    plan, groups, order, n_col = opts["plan"], opts["groups"], opts["order"], opts["n_col"]
    lefts, refs = refs[: opts["lefts"]], refs[opts["lefts"] :]
    sources, refs = refs[: opts["outs"] * len(plan)], refs[opts["outs"] * len(plan) :]
    before = refs[0] if opts["before"] else None
    *outs, right, sems = refs[opts["before"] + opts["held"] :]
    row, me = where[0], where[1]
    sub = right.shape[2] // 2
    depth = right.shape[1] // n_col
    first = groups[0][0] * sub
    third = pl.program_id(1)

    def copies(t, phase):
        for s, (low, high, step) in enumerate(plan):
            source = sources[t * len(plan) + s]
            if len(plan) == 1:
                for c in range(n_col):
                    copy = pltpu.make_async_copy(
                        source.at[pl.ds(c * sub * THIRDS + first, depth)],
                        right.at[t, pl.ds(c * depth, depth)],
                        sems.at[t, c],
                    )
                    copy.start() if phase == 0 else copy.wait()
                continue

            @pl.when((row >= low) & (row <= high))
            def _(s=s, step=step, source=source):
                start = pl.multiple_of((row + step) * depth, 32)
                copy = pltpu.make_async_copy(
                    source.at[pl.ds(first, depth)], right.at[t, pl.ds(start, depth)], sems.at[t, s]
                )
                copy.start() if phase == 0 else copy.wait()

    for t in range(opts["outs"]):

        @pl.when((pl.program_id(0) == 0) & (third == 0))
        def _(t=t):
            copies(t, 0)

    for t in range(opts["outs"]):

        @pl.when((pl.program_id(0) == 0) & (third == t))
        def _(t=t):
            copies(t, 1)

    tile = lefts[0].shape[-2]
    by_real = jnp.zeros((tile, 2 * sub), F32)
    by_imag = jnp.zeros((tile, 2 * sub), F32)
    for c in range(n_col):
        if opts["by_xor"]:
            slices = [lefts[g * n_col + c][...] for g in range(len(groups))]
            start = pl.multiple_of((me ^ c) * depth, 32)
        else:
            slices = [
                left[c, :, 2 * k * sub : 2 * (k + 1) * sub] for left, group in zip(lefts, groups) for k in range(len(group))
            ]
            start = c * depth
        for k, left in enumerate(slices):
            rows = right[third, pl.ds(start + k * sub, sub), :]
            by_real += jnp.dot(left[:, :sub], rows, preferred_element_type=F32)
            by_imag += jnp.dot(left[:, sub:], rows, preferred_element_type=F32)
    real = by_real[:, :sub] - by_imag[:, sub:]
    imag = by_real[:, sub:] + by_imag[:, :sub]
    if before is not None:
        real = real + before[:, :sub]
        imag = imag + before[:, sub:]
    if order is None:
        outs[0][:, :sub] = real
        outs[0][:, sub:] = imag
        return
    real = (real * opts["weight"]).astype(BF16)
    imag = (imag * opts["weight"]).astype(BF16)
    outs[0][0, 0] = real
    outs[0][0, 1] = imag
    if len(outs) > 1:
        outs[1][:, :sub] = real
        outs[1][:, sub:] = imag


def complex_product(where, lefts, plan, rights, shape, held, at, before=None, piece_at=(0, 1)):
    groups = [group for _, group in lefts]
    by_xor = isinstance(lefts[0][0], list)
    arrays = [a for pieces, _ in lefts for a in pieces] if by_xor else [a for a, _ in lefts]
    n_col = len(lefts[0][0]) if by_xor else arrays[0].shape[0]
    rows = arrays[0].shape[-2]
    tile = 256 if rows % 256 == 0 else rows
    wide = rights[0][0].shape[1]
    sub = wide // 2
    count = len(rights)
    order = None
    if at is None:
        out_specs = [pl.BlockSpec((tile, wide), lambda i, j, s: (i, j))]
        out_shape = [jax.ShapeDtypeStruct((rows, count * wide), F32)]
    else:
        order, f, first = at
        out_specs = [pl.BlockSpec((1, 2, tile, sub), lambda i, j, s: (order, f, i, first + j))]
        out_shape = [jax.ShapeDtypeStruct(shape, BF16)]
        if order == 0:
            which, of = piece_at
            out_specs.append(pl.BlockSpec((tile, wide), lambda i, j, s: (i, which + j)))
            out_shape.append(jax.ShapeDtypeStruct((rows, of * wide), BF16))
    if by_xor:
        in_specs = [pl.BlockSpec((tile, wide), lambda i, j, s: (i, 0)) for a in arrays]
    else:
        in_specs = [pl.BlockSpec((n_col, tile, a.shape[2]), lambda i, j, s: (0, i, 0)) for a in arrays]
    sources = [a for found in rights for a in found]
    in_specs += [pl.BlockSpec(memory_space=pl.ANY)] * len(sources)
    args = [*arrays, *sources]
    if before is not None:
        in_specs.append(pl.BlockSpec((tile, wide), lambda i, j, s: (i, j)))
        args.append(before)
    aliases = {1 + len(args) + k: k for k in range(len(held))}
    in_specs += [pl.BlockSpec(memory_space=pl.ANY)] * len(held)
    depth = sum(len(g) for g in groups) * n_col * sub
    opts = dict(
        plan=plan,
        groups=groups,
        order=order,
        n_col=n_col,
        lefts=len(arrays),
        outs=count,
        by_xor=by_xor,
        weight=1.0 / math.sqrt(2.0 * NS),
        before=int(before is not None),
        held=len(held),
    )
    return pl.pallas_call(
        functools.partial(product_kernel, opts),
        grid_spec=pltpu.PrefetchScalarGridSpec(
            num_scalar_prefetch=1,
            grid=(rows // tile, count),
            in_specs=in_specs,
            out_specs=out_specs,
            scratch_shapes=[
                pltpu.VMEM((count, depth, wide), BF16),
                pltpu.SemaphoreType.DMA((count, max(len(plan), n_col))),
            ],
        ),
        out_shape=out_shape,
        input_output_aliases=aliases,
        compiler_params=pltpu.CompilerParams(vmem_limit_bytes=48 * 2**20),
        cost_estimate=pl.CostEstimate(flops=1000, bytes_accessed=1000, transcendentals=0),
    )(where, *args, *held)


def per_device(acq_data, grid_row, counts):
    n_row = lax.axis_size("row")
    n_col = lax.axis_size("col")
    own_cap, planes, order = acq_data.shape
    block_rows = order // n_row
    tile_cols = order // n_col
    cap = own_cap // n_row
    slots = n_row * cap
    wide = 2 * tile_cols // THIRDS
    everything = tuple(range(THIRDS))

    slot_index = jnp.arange(own_cap, dtype=jnp.int32)
    block = jnp.where(slot_index < counts[0], grid_row // block_rows, n_row)
    earlier = (block[None, :] == block[:, None]) & (slot_index[None, :] < slot_index[:, None])
    rank = jnp.sum(earlier.astype(jnp.int32), axis=1)
    leaving = jnp.where(block < n_row, block * cap + rank, -1)
    hit = jnp.arange(slots, dtype=jnp.int32)[:, None] == leaving[None, :]
    spots = jnp.sum(jnp.where(hit, (grid_row % block_rows)[None, :] + 1, 0), axis=1) - 1
    picker = hit.astype(BF16)
    data = jnp.transpose(acq_data, (1, 0, 2))
    line = n_row <= 4 and block_rows == tile_cols
    plan = [(0, n_row - 1, 0)]
    if line:
        for k in range(1, n_row):
            plan += [(0, n_row - 1 - k, k), (k, n_row - 1, -k)]

    my_row = lax.axis_index("row")
    keys = [(f, j) for f in range(FREQ) for j in everything]
    known = lax.all_gather(spots, ("row", "col"), axis=0).reshape(n_row * n_col, n_row, cap)
    places = lax.dynamic_index_in_dim(known, my_row, axis=1, keepdims=False).reshape(-1)
    placer = (jnp.arange(block_rows, dtype=jnp.int32)[:, None] == places[None, :]).astype(BF16)

    pieces, pairs, rights, lefts = {}, {}, {}, [[], []]
    for f, group in ((0, (0,)), (0, everything[1:]), (1, everything)):
        sent = bin_rows(picker, data, f, group, n_row, n_col)
        got = lax.all_to_all(
            sent.reshape(n_row * n_col, cap, wide * len(group)), ("row", "col"), split_axis=0, concat_axis=0, tiled=True
        ).reshape(-1, wide * len(group))
        if line and f == 0 and group[0]:
            got = after(got, pairs[0, 0, 1])
        tile = jnp.dot(placer, got, preferred_element_type=F32).astype(BF16)
        lefts[f].append((lax.all_gather(tile, "col", axis=0), group))
        for k, j in enumerate(group):
            piece = pieces[f, j] = tile[:, k * wide : (k + 1) * wide]
            if line:
                pairs[f, j, 1] = hop((piece, piece), 1, n_row)
    if line:
        for f in range(FREQ):
            for k in range(2, n_row):
                for j in everything:
                    begun = pairs[f, j, k - 1]
                    if f == 0 and k == 2 and j:
                        begun = after(begun, got)
                    if f == 0 and k == n_row - 1 and j == THIRDS - 1:
                        begun = after(begun, pairs[1, 0, 1])
                    if f == 1 and j + 1 < THIRDS:
                        begun = after(begun, pairs[f, j + 1, k - 1])
                    pairs[f, j, k] = hop(begun, k, n_row)
    for key in keys:
        if line:
            rights[key] = [pieces[key]] + [a for k in range(1, n_row) for a in pairs[(*key, k)]]
        else:
            rights[key] = [lax.all_gather(pieces[key], "row", axis=0, tiled=True)]

    where = jnp.stack([my_row, lax.axis_index("col")]).astype(jnp.int32)
    product = functools.partial(complex_product, where)
    shape = (2, planes, block_rows, tile_cols)
    held = ()
    if line:
        rights[0, THIRDS - 1][0] = after(rights[0, THIRDS - 1][0], pairs[1, 1, 1])
    for j in everything:
        held = product(lefts[0], plan, [rights[0, j]], shape, tuple(held), (0, 0, j), piece_at=(j, THIRDS))
    result, piece = held
    gathered = [(lax.all_gather(piece, "col", axis=0), everything)]
    for j in everything:
        (result,) = product(gathered, plan, [rights[0, j]], shape, (result,), (1, 0, j))
    gathered = []
    for j in everything:
        result, piece = product(lefts[1], plan, [rights[1, j]], shape, (result,), (0, 1, j))
        if gathered:
            piece = after(piece, gathered[-1][0][n_col // 2])
        gathered.append((gather_cols(piece, n_col), (j,)))
    final = [rights[1, j] for j in everything]
    (sums,) = product(gathered[:-1], plan, final, shape, (), None)
    return product(gathered[-1:], plan, final, shape, (result,), (1, 1, 0), before=sums)[0]


def solution(mesh):
    placed = (
        P(("groups", "row", "col"), None, None),
        P(("groups", "row", "col")),
        P(("groups", "row", "col")),
    )
    return jax.shard_map(
        per_device,
        mesh=mesh,
        in_specs=placed,
        out_specs=P("groups", None, "row", "col"),
        check_vma=False,
    )
```

```python
import functools
import math

import jax
import jax.numpy as jnp
from jax import lax
from jax.experimental import pallas as pl
from jax.experimental.pallas import tpu as pltpu
from jax.sharding import PartitionSpec as P

NS = 3072
FREQ = 2
THIRDS = 3
BF16 = jnp.bfloat16
F32 = jnp.float32


def hop(pair, k, n_row):
    down = [(r, r - 1) for r in range(1, n_row) if r + k - 1 < n_row]
    up = [(r, r + 1) for r in range(n_row - 1) if r - k + 1 >= 0]
    return lax.ppermute(pair[0], "row", down), lax.ppermute(pair[1], "row", up)


CHEAP = pl.CostEstimate(flops=1000, bytes_accessed=1000, transcendentals=0)


def bin_kernel(picker, data, out):
    n_row, cap = out.shape[0], out.shape[2]
    cols = data.shape[2]
    for p in range(2):
        rows = jnp.dot(picker[...], data[p], preferred_element_type=F32).astype(BF16)
        for b in range(n_row):
            out[b, 0, :, p * cols : (p + 1) * cols] = rows[b * cap : (b + 1) * cap]


def bin_rows(picker, data, f, n_row, n_col):
    planes, own_cap, order = data.shape
    cap = picker.shape[0] // n_row
    cols = order // n_col
    return pl.pallas_call(
        bin_kernel,
        grid=(n_col,),
        in_specs=[
            pl.BlockSpec(picker.shape, lambda c: (0, 0)),
            pl.BlockSpec((2, own_cap, cols), lambda c: (f, 0, c)),
        ],
        out_specs=pl.BlockSpec((n_row, 1, cap, 2 * cols), lambda c: (0, c, 0, 0)),
        out_shape=jax.ShapeDtypeStruct((n_row, n_col, cap, 2 * cols), BF16),
        compiler_params=pltpu.CompilerParams(vmem_limit_bytes=24 * 2**20),
        cost_estimate=CHEAP,
    )(picker, data)


def place_kernel(placer, got, tile, *thirds):
    rows = jnp.dot(placer[...], got[...], preferred_element_type=F32).astype(BF16)
    tile[0] = rows
    for j, third in enumerate(thirds):
        sub = third.shape[2]
        third[0] = rows[:, j * sub : (j + 1) * sub]


def place_rows(placer, got, split):
    block_rows, arrived = placer.shape
    cols = got.shape[1] // 2
    sizes = [cols] + [cols // THIRDS] * (THIRDS if split else 0)
    return pl.pallas_call(
        place_kernel,
        grid=(2,),
        in_specs=[
            pl.BlockSpec(placer.shape, lambda p: (0, 0)),
            pl.BlockSpec((arrived, cols), lambda p: (0, p)),
        ],
        out_specs=[pl.BlockSpec((1, block_rows, n), lambda p: (p, 0, 0)) for n in sizes],
        out_shape=[jax.ShapeDtypeStruct((2, block_rows, n), BF16) for n in sizes],
        compiler_params=pltpu.CompilerParams(vmem_limit_bytes=32 * 2**20),
        cost_estimate=CHEAP,
    )(placer, got)


def after(value, earlier):
    return lax.optimization_barrier((value, earlier))[0]


def gather_cols(piece, n_col):
    held = {0: piece}
    bit = n_col // 2
    while bit:
        pairs = [(c, c ^ bit) for c in range(n_col)]
        arrived = {d ^ bit: lax.ppermute(a, "col", pairs) for d, a in held.items()}
        held.update(arrived)
        bit //= 2
    return [held[d] for d in range(n_col)]


def product_kernel(opts, where, *refs):
    plan, groups, order, n_col = opts["plan"], opts["groups"], opts["order"], opts["n_col"]
    per_third = opts["per_third"]
    lefts, refs = refs[: len(groups)], refs[len(groups) :]
    sources, refs = refs[: opts["sources"]], refs[opts["sources"] :]
    before = refs[0] if opts["before"] else None
    *outs, right, total, sems = refs[opts["before"] + opts["held"] :]
    row, me = where[0], where[1]
    sub = right.shape[2] // 2
    depth = right.shape[1] // n_col
    first = groups[0][0] * sub
    third, step = pl.program_id(0), pl.program_id(1)

    def copy_of(source, from_row, t, p, block):
        lanes = pl.ds(0 if per_third else (opts["third"] + t) * sub, sub)
        start = block * depth if isinstance(block, int) else pl.multiple_of(block * depth, 32)
        return pltpu.make_async_copy(
            source.at[p, pl.ds(from_row, depth), lanes],
            right.at[t, pl.ds(start, depth), pl.ds(p * sub, sub)],
            sems.at[t, p, block],
        )

    @pl.when((third == 0) & (step == 0))
    def _():
        for t in range(right.shape[0]):
            for s, (low, high, up) in enumerate(plan):
                source = sources[t * len(plan) + s if per_third else s]
                if len(plan) == 1:
                    for c in range(n_col):
                        for p in range(2):
                            copy_of(source, c * sub * THIRDS + first, t, p, c).start()
                    continue

                @pl.when((row >= low) & (row <= high))
                def _(source=source, up=up, t=t):
                    for p in range(2):
                        copy_of(source, first, t, p, row + up).start()

    block = me ^ step if opts["by_xor"] else step
    for t in range(right.shape[0]):

        @pl.when(third == t)
        def _(t=t):
            for p in range(2):
                copy_of(sources[0], first, t, p, block).wait()

    real = imag = None
    start = block * depth
    for left, group in zip(lefts, groups):
        deep = len(group) * sub
        rows = right[third, pl.ds(pl.multiple_of(start, 32), deep), :]
        start = start + deep
        by_real = jnp.dot(left[0, 0], rows, preferred_element_type=F32)
        by_imag = jnp.dot(left[0, 1], rows, preferred_element_type=F32)
        real_now = by_real[:, :sub] - by_imag[:, sub:]
        imag_now = by_real[:, sub:] + by_imag[:, :sub]
        real = real_now if real is None else real + real_now
        imag = imag_now if imag is None else imag + imag_now

    @pl.when(step == 0)
    def _():
        total[0] = real if before is None else real + before[0]
        total[1] = imag if before is None else imag + before[1]

    @pl.when(step > 0)
    def _():
        total[0] += real
        total[1] += imag

    @pl.when(step == n_col - 1)
    def _():
        for p in range(2):
            if order is None:
                outs[0][p] = total[p]
                continue
            value = (total[p] * opts["weight"]).astype(BF16)
            outs[0][0, p] = value
            if len(outs) > 1:
                outs[1][p] = value


def complex_product(where, lefts, plan, sources, per_third, count, shape, held, at, before=None, piece_at=(0, 1), by_xor=False):
    groups = [group for _, group in lefts]
    arrays = [a for a, _ in lefts]
    n_col, _, rows, lanes = arrays[0].shape
    sub = lanes // len(groups[0])
    order, third = None, 0
    if at is None:
        out_specs = [pl.BlockSpec((2, rows, sub), lambda t, c, s: (0, 0, t))]
        out_shape = [jax.ShapeDtypeStruct((2, rows, count * sub), F32)]
    else:
        order, f, third = at
        out_specs = [pl.BlockSpec((1, 2, rows, sub), lambda t, c, s: (order, f, 0, third + t))]
        out_shape = [jax.ShapeDtypeStruct(shape, BF16)]
        if order == 0:
            which, of = piece_at
            out_specs.append(pl.BlockSpec((2, rows, sub), lambda t, c, s: (0, 0, which + t)))
            out_shape.append(jax.ShapeDtypeStruct((2, rows, of * sub), BF16))
    in_specs = [pl.BlockSpec((1, 2, rows, a.shape[3]), lambda t, c, s: (c, 0, 0, 0)) for a in arrays]
    in_specs += [pl.BlockSpec(memory_space=pl.ANY)] * len(sources)
    args = [*arrays, *sources]
    if before is not None:
        in_specs.append(pl.BlockSpec((2, rows, sub), lambda t, c, s: (0, 0, t)))
        args.append(before)
    aliases = {1 + len(args) + k: k for k in range(len(held))}
    in_specs += [pl.BlockSpec(memory_space=pl.ANY)] * len(held)
    depth = sum(len(g) for g in groups) * n_col * sub
    opts = dict(
        plan=plan,
        groups=groups,
        order=order,
        third=third,
        n_col=n_col,
        sources=len(sources),
        per_third=per_third,
        by_xor=by_xor,
        weight=1.0 / math.sqrt(2.0 * NS),
        before=int(before is not None),
        held=len(held),
    )
    return pl.pallas_call(
        functools.partial(product_kernel, opts),
        grid_spec=pltpu.PrefetchScalarGridSpec(
            num_scalar_prefetch=1,
            grid=(count, n_col),
            in_specs=in_specs,
            out_specs=out_specs,
            scratch_shapes=[
                pltpu.VMEM((count, depth, 2 * sub), BF16),
                pltpu.VMEM((2, rows, sub), F32),
                pltpu.SemaphoreType.DMA((count, 2, n_col)),
            ],
        ),
        out_shape=out_shape,
        input_output_aliases=aliases,
        compiler_params=pltpu.CompilerParams(vmem_limit_bytes=48 * 2**20),
        cost_estimate=CHEAP,
    )(where, *args, *held)


def per_device(acq_data, grid_row, counts):
    n_row = lax.axis_size("row")
    n_col = lax.axis_size("col")
    own_cap, planes, order = acq_data.shape
    block_rows = order // n_row
    tile_cols = order // n_col
    cap = own_cap // n_row
    slots = n_row * cap
    wide = 2 * tile_cols // THIRDS
    everything = tuple(range(THIRDS))

    slot_index = jnp.arange(own_cap, dtype=jnp.int32)
    block = jnp.where(slot_index < counts[0], grid_row // block_rows, n_row)
    earlier = (block[None, :] == block[:, None]) & (slot_index[None, :] < slot_index[:, None])
    rank = jnp.sum(earlier.astype(jnp.int32), axis=1)
    leaving = jnp.where(block < n_row, block * cap + rank, -1)
    hit = jnp.arange(slots, dtype=jnp.int32)[:, None] == leaving[None, :]
    spots = jnp.sum(jnp.where(hit, (grid_row % block_rows)[None, :] + 1, 0), axis=1) - 1
    picker = hit.astype(BF16)
    data = jnp.transpose(acq_data, (1, 0, 2))
    line = n_row <= 4 and block_rows == tile_cols
    plan = [(0, n_row - 1, 0)]
    if line:
        for k in range(1, n_row):
            plan += [(0, n_row - 1 - k, k), (k, n_row - 1, -k)]

    my_row = lax.axis_index("row")
    keys = [(f, j) for f in range(FREQ) for j in everything]
    known = lax.all_gather(spots, ("row", "col"), axis=0).reshape(n_row * n_col, n_row, cap)
    places = lax.dynamic_index_in_dim(known, my_row, axis=1, keepdims=False).reshape(-1)
    placer = (jnp.arange(block_rows, dtype=jnp.int32)[:, None] == places[None, :]).astype(BF16)

    tiles, thirds, lefts = [], [], []
    for f in range(FREQ):
        sent = bin_rows(picker, data, f, n_row, n_col)
        got = lax.all_to_all(
            sent.reshape(n_row * n_col, cap, 2 * tile_cols), ("row", "col"), split_axis=0, concat_axis=0, tiled=True
        ).reshape(-1, 2 * tile_cols)
        tile, *cut = place_rows(placer, got, line and f == 1)
        tiles.append(tile)
        thirds.append(cut)
        lefts.append((lax.all_gather(tile, "col", axis=0), everything))

    if line:
        pair = hop((tiles[0], tiles[0]), 1, n_row)
        right0 = [tiles[0], *pair]
        for k in range(2, n_row):
            pair = hop(after(pair, got) if k == 2 else pair, k, n_row)
            right0 += list(pair)
        hops = [[hop((a, a), 1, n_row) for a in thirds[1]]]
        for k in range(2, n_row):
            begun = hops[-1]
            hops.append([])
            for j in everything:
                hops[-1].append(hop(begun[j], k, n_row))
        right1 = [[thirds[1][j]] + [a for of in hops for a in of[j]] for j in everything]
    else:
        right0, right1 = ([lax.all_gather(tile, "row", axis=1, tiled=True)] for tile in tiles)

    where = jnp.stack([my_row, lax.axis_index("col")]).astype(jnp.int32)
    shape = (2, planes, block_rows, tile_cols)

    def product(lefts, f, at, held, count=1, **rest):
        first = 0 if at is None else at[2]
        sources, per_third = right0, False
        if f == 1:
            sources, per_third = right1, line
            if line:
                sources = [a for j in range(first, first + count) for a in right1[j]]
        return complex_product(where, lefts, plan, sources, per_third, count, shape, tuple(held), at, **rest)

    held = ()
    gate = where
    for j in everything:
        if line:
            gate = (hops[0], lefts[1][0]) if j == 0 else hops[1][0]
            right0[0] = after(right0[0], gate)
        held = product([lefts[0]], 0, (0, 0, j), held, piece_at=(j, THIRDS))
    result, piece = held
    left0 = [(lax.all_gather(piece, "col", axis=0), everything)]
    left1 = []
    arrived = None
    for j in everything:
        if j == THIRDS - 1:
            (result,) = product(left0, 0, (1, 0, 0), (result,), count=THIRDS)
        result, piece = product([lefts[1]], 1, (0, 1, j), (result,))
        if arrived is not None:
            piece = after(piece, arrived)
        found = gather_cols(piece, n_col)
        arrived = found[n_col // 2]
        left1.append((jnp.stack(found), (j,)))
    (sums,) = product(left1[:-1], 1, None, (), count=THIRDS, by_xor=True)
    return product(left1[-1:], 1, (1, 1, 0), (result,), count=THIRDS, before=sums, by_xor=True)[0]


def solution(mesh):
    placed = (
        P(("groups", "row", "col"), None, None),
        P(("groups", "row", "col")),
        P(("groups", "row", "col")),
    )
    return jax.shard_map(
        per_device,
        mesh=mesh,
        in_specs=placed,
        out_specs=P("groups", None, "row", "col"),
        check_vma=False,
    )
```

```python
import functools
import math

import jax
import jax.numpy as jnp
from jax import lax
from jax.experimental import pallas as pl
from jax.experimental.pallas import tpu as pltpu
from jax.sharding import PartitionSpec as P

NS = 3072
FREQ = 2
THIRDS = 3
BF16 = jnp.bfloat16
F32 = jnp.float32


def hop(pair, k, n_row):
    down = [(r, r - 1) for r in range(1, n_row) if r + k - 1 < n_row]
    up = [(r, r + 1) for r in range(n_row - 1) if r - k + 1 >= 0]
    return lax.ppermute(pair[0], "row", down), lax.ppermute(pair[1], "row", up)


CHEAP = pl.CostEstimate(flops=1000, bytes_accessed=1000, transcendentals=0)


def bin_kernel(picker, data, out):
    n_row, cap = out.shape[0], out.shape[2]
    cols = data.shape[2]
    for p in range(2):
        rows = jnp.dot(picker[...], data[p], preferred_element_type=F32).astype(BF16)
        for b in range(n_row):
            out[b, 0, :, p * cols : (p + 1) * cols] = rows[b * cap : (b + 1) * cap]


def bin_rows(picker, data, f, n_row, n_col):
    planes, own_cap, order = data.shape
    cap = picker.shape[0] // n_row
    cols = order // n_col
    return pl.pallas_call(
        bin_kernel,
        grid=(n_col,),
        in_specs=[
            pl.BlockSpec(picker.shape, lambda c: (0, 0)),
            pl.BlockSpec((2, own_cap, cols), lambda c: (f, 0, c)),
        ],
        out_specs=pl.BlockSpec((n_row, 1, cap, 2 * cols), lambda c: (0, c, 0, 0)),
        out_shape=jax.ShapeDtypeStruct((n_row, n_col, cap, 2 * cols), BF16),
        compiler_params=pltpu.CompilerParams(vmem_limit_bytes=24 * 2**20),
        cost_estimate=CHEAP,
    )(picker, data)


def place_kernel(placer, got, tile, *thirds):
    rows = jnp.dot(placer[...], got[...], preferred_element_type=F32).astype(BF16)
    tile[0] = rows
    for j, third in enumerate(thirds):
        sub = third.shape[2]
        third[0] = rows[:, j * sub : (j + 1) * sub]


def place_rows(placer, got, split):
    block_rows, arrived = placer.shape
    cols = got.shape[1] // 2
    sizes = [cols] + [cols // THIRDS] * (THIRDS if split else 0)
    return pl.pallas_call(
        place_kernel,
        grid=(2,),
        in_specs=[
            pl.BlockSpec(placer.shape, lambda p: (0, 0)),
            pl.BlockSpec((arrived, cols), lambda p: (0, p)),
        ],
        out_specs=[pl.BlockSpec((1, block_rows, n), lambda p: (p, 0, 0)) for n in sizes],
        out_shape=[jax.ShapeDtypeStruct((2, block_rows, n), BF16) for n in sizes],
        compiler_params=pltpu.CompilerParams(vmem_limit_bytes=32 * 2**20),
        cost_estimate=CHEAP,
    )(placer, got)


def after(value, earlier):
    return lax.optimization_barrier((value, earlier))[0]


def gather_cols(piece, n_col, second_after=None):
    held = {0: piece}
    bit = n_col // 2
    while bit:
        if second_after is not None and len(held) == 2:
            held = {d: after(a, second_after) for d, a in held.items()}
        pairs = [(c, c ^ bit) for c in range(n_col)]
        arrived = {d ^ bit: lax.ppermute(a, "col", pairs) for d, a in held.items()}
        held.update(arrived)
        bit //= 2
    return [held[d] for d in range(n_col)]


def product_kernel(opts, where, *refs):
    plan, groups, order, n_col, count = (opts[k] for k in ("plan", "groups", "order", "n_col", "count"))
    per_third, by_xor = opts["per_third"], opts["by_xor"]
    arrays, refs = refs[: opts["lefts"]], refs[opts["lefts"] :]
    sources, refs = refs[: opts["sources"]], refs[opts["sources"] :]
    before = refs[0] if opts["before"] else None
    *outs, left, right, total, left_sems, sems = refs[opts["before"] + opts["held"] :]
    row, me = where[0], where[1]
    sub = right.shape[2] // 2
    depth = right.shape[1] // n_col
    first = groups[0][0] * sub
    step, third = pl.program_id(0), pl.program_id(1)

    def left_copies(c):
        found, at = [], 0
        for g, group in enumerate(groups):
            source = arrays[g * n_col + c] if by_xor else arrays[g].at[c]
            lanes = pl.ds(at, len(group) * sub)
            found.append(pltpu.make_async_copy(source, left.at[c, :, :, lanes], left_sems.at[g, c]))
            at += len(group) * sub
        return found

    def copy_of(source, from_row, t, p, block):
        lanes = pl.ds(0 if per_third else (opts["third"] + t) * sub, sub)
        start = block * depth if isinstance(block, int) else pl.multiple_of(block * depth, 32)
        return pltpu.make_async_copy(
            source.at[p, pl.ds(from_row, depth), lanes],
            right.at[t, pl.ds(start, depth), pl.ds(p * sub, sub)],
            sems.at[t, p, block],
        )

    @pl.when((third == 0) & (step == 0))
    def _():
        for copy in left_copies(0):
            copy.start()
        for t in range(count):
            for s, (low, high, up) in enumerate(plan):
                source = sources[t * len(plan) + s if per_third else s]
                if len(plan) == 1:
                    for c in range(n_col):
                        for p in range(2):
                            copy_of(source, c * sub * THIRDS + first, t, p, c).start()
                    continue

                @pl.when((row >= low) & (row <= high))
                def _(source=source, up=up, t=t):
                    for p in range(2):
                        copy_of(source, first, t, p, row + up).start()

        for c in range(1, n_col):
            for copy in left_copies(c):
                copy.start()

    for c in range(n_col):

        @pl.when((third == 0) & (step == c))
        def _(c=c):
            for copy in left_copies(c):
                copy.wait()

    block = me ^ step if by_xor else step
    for t in range(count):

        @pl.when(third == t)
        def _(t=t):
            for p in range(2):
                copy_of(sources[0], first, t, p, block).wait()

    rows = right[third, pl.ds(pl.multiple_of(block * depth, 32), depth), :]
    by_real = jnp.dot(left[step, 0], rows, preferred_element_type=F32)
    by_imag = jnp.dot(left[step, 1], rows, preferred_element_type=F32)
    real = by_real[:, :sub] - by_imag[:, sub:]
    imag = by_real[:, sub:] + by_imag[:, :sub]

    @pl.when(step == 0)
    def _():
        total[third, 0] = real if before is None else real + before[0]
        total[third, 1] = imag if before is None else imag + before[1]

    @pl.when(step > 0)
    def _():
        total[third, 0] += real
        total[third, 1] += imag

    @pl.when(step == n_col - 1)
    def _():
        for p in range(2):
            if order is None:
                outs[0][p] = total[third, p]
                continue
            value = (total[third, p] * opts["weight"]).astype(BF16)
            outs[0][0, p] = value
            if len(outs) > 1:
                outs[1][p] = value


def complex_product(where, lefts, plan, sources, per_third, count, shape, held, at, before=None):
    groups = [group for _, group in lefts]
    by_xor = isinstance(lefts[0][0], list)
    arrays = [a for pieces, _ in lefts for a in pieces] if by_xor else [a for a, _ in lefts]
    n_col = len(lefts[0][0]) if by_xor else arrays[0].shape[0]
    rows = arrays[0].shape[-2]
    sub = arrays[0].shape[-1] // len(groups[0])
    lanes = sum(len(g) for g in groups) * sub
    order, third = None, 0

    def late(c, t):
        return jnp.where(c == n_col - 1, t, 0)

    if at is None:
        out_specs = [pl.BlockSpec((2, rows, sub), lambda c, t, s: (0, 0, late(c, t)))]
        out_shape = [jax.ShapeDtypeStruct((2, rows, count * sub), F32)]
    else:
        order, f, third = at
        out_specs = [pl.BlockSpec((1, 2, rows, sub), lambda c, t, s: (order, f, 0, third + late(c, t)))]
        out_shape = [jax.ShapeDtypeStruct(shape, BF16)]
        if order == 0:
            out_specs.append(pl.BlockSpec((2, rows, sub), lambda c, t, s: (0, 0, late(c, t))))
            out_shape.append(jax.ShapeDtypeStruct((2, rows, count * sub), BF16))
    in_specs = [pl.BlockSpec(memory_space=pl.ANY)] * (len(arrays) + len(sources))
    args = [*arrays, *sources]
    if before is not None:
        in_specs.append(pl.BlockSpec((2, rows, sub), lambda c, t, s: (0, 0, jnp.where(c == 0, t, count - 1))))
        args.append(before)
    aliases = {1 + len(args) + k: k for k in range(len(held))}
    in_specs += [pl.BlockSpec(memory_space=pl.ANY)] * len(held)
    opts = dict(
        plan=plan,
        groups=groups,
        order=order,
        third=third,
        n_col=n_col,
        count=count,
        lefts=len(arrays),
        sources=len(sources),
        per_third=per_third,
        by_xor=by_xor,
        weight=1.0 / math.sqrt(2.0 * NS),
        before=int(before is not None),
        held=len(held),
    )
    return pl.pallas_call(
        functools.partial(product_kernel, opts),
        grid_spec=pltpu.PrefetchScalarGridSpec(
            num_scalar_prefetch=1,
            grid=(n_col, count),
            in_specs=in_specs,
            out_specs=out_specs,
            scratch_shapes=[
                pltpu.VMEM((n_col, 2, rows, lanes), BF16),
                pltpu.VMEM((count, lanes * n_col, 2 * sub), BF16),
                pltpu.VMEM((count, 2, rows, sub), F32),
                pltpu.SemaphoreType.DMA((len(groups), n_col)),
                pltpu.SemaphoreType.DMA((count, 2, n_col)),
            ],
        ),
        out_shape=out_shape,
        input_output_aliases=aliases,
        compiler_params=pltpu.CompilerParams(vmem_limit_bytes=(44 if count > 1 else 24) * 2**20),
        cost_estimate=CHEAP,
    )(where, *args, *held)


def per_device(acq_data, grid_row, counts):
    n_row = lax.axis_size("row")
    n_col = lax.axis_size("col")
    own_cap, planes, order = acq_data.shape
    block_rows = order // n_row
    tile_cols = order // n_col
    cap = own_cap // n_row
    slots = n_row * cap
    wide = 2 * tile_cols // THIRDS
    everything = tuple(range(THIRDS))

    slot_index = jnp.arange(own_cap, dtype=jnp.int32)
    block = jnp.where(slot_index < counts[0], grid_row // block_rows, n_row)
    earlier = (block[None, :] == block[:, None]) & (slot_index[None, :] < slot_index[:, None])
    rank = jnp.sum(earlier.astype(jnp.int32), axis=1)
    leaving = jnp.where(block < n_row, block * cap + rank, -1)
    hit = jnp.arange(slots, dtype=jnp.int32)[:, None] == leaving[None, :]
    spots = jnp.sum(jnp.where(hit, (grid_row % block_rows)[None, :] + 1, 0), axis=1) - 1
    picker = hit.astype(BF16)
    data = jnp.transpose(acq_data, (1, 0, 2))
    line = n_row <= 4 and block_rows == tile_cols
    plan = [(0, n_row - 1, 0)]
    if line:
        for k in range(1, n_row):
            plan += [(0, n_row - 1 - k, k), (k, n_row - 1, -k)]

    my_row = lax.axis_index("row")
    keys = [(f, j) for f in range(FREQ) for j in everything]
    known = lax.all_gather(spots, ("row", "col"), axis=0).reshape(n_row * n_col, n_row, cap)
    places = lax.dynamic_index_in_dim(known, my_row, axis=1, keepdims=False).reshape(-1)
    placer = (jnp.arange(block_rows, dtype=jnp.int32)[:, None] == places[None, :]).astype(BF16)

    tiles, thirds, lefts = [], [], []
    pair = None
    for f in range(FREQ):
        sent = bin_rows(picker, data, f, n_row, n_col)
        got = lax.all_to_all(
            sent.reshape(n_row * n_col, cap, 2 * tile_cols), ("row", "col"), split_axis=0, concat_axis=0, tiled=True
        ).reshape(-1, 2 * tile_cols)
        if pair is not None:
            got, pair = lax.optimization_barrier((got, pair))
        tile, *cut = place_rows(placer, got, line and f == 1)
        if line and f == 0:
            pair = hop((tile, tile), 1, n_row)
        tiles.append(tile)
        thirds.append(cut)
        lefts.append((lax.all_gather(tile, "col", axis=0), everything))

    if line:
        right0 = [tiles[0], *pair]
        for k in range(2, n_row):
            pair = hop(pair, k, n_row)
            right0 += list(pair)
        hops = [[hop((a, a), 1, n_row) for a in thirds[1]]]
        for k in range(2, n_row):
            begun = hops[-1]
            hops.append([hop(begun[j], k, n_row) for j in everything])
        right1 = [[thirds[1][j]] + [a for of in hops for a in of[j]] for j in everything]
        right0[0] = after(right0[0], (hops[0], hops[1][0], lefts[1][0]))
    else:
        right0, right1 = ([lax.all_gather(tile, "row", axis=1, tiled=True)] for tile in tiles)

    where = jnp.stack([my_row, lax.axis_index("col")]).astype(jnp.int32)
    shape = (2, planes, block_rows, tile_cols)

    def product(lefts, f, at, held, count=THIRDS, **rest):
        first = 0 if at is None else at[2]
        sources, per_third = right0, False
        if f == 1:
            sources, per_third = right1, line
            if line:
                sources = [a for j in range(first, first + count) for a in right1[j]]
        return complex_product(where, lefts, plan, sources, per_third, count, shape, tuple(held), at, **rest)

    result, piece = product([lefts[0]], 0, (0, 0, 0), ())
    found = gather_cols(piece, n_col, hops[1][1:] if line else None)
    arrived = found[n_col // 2]
    (result,) = product([(found, everything)], 0, (1, 0, 0), (result,))
    left1 = []
    for j in everything:
        result, piece = product([lefts[1]], 1, (0, 1, j), (result,), count=1)
        found = gather_cols(after(piece, arrived), n_col)
        arrived = found[n_col // 2]
        left1.append((found, (j,)))
    (sums,) = product(left1[:-1], 1, None, ())
    return product(left1[-1:], 1, (1, 1, 0), (result,), before=sums)[0]


def solution(mesh):
    placed = (
        P(("groups", "row", "col"), None, None),
        P(("groups", "row", "col")),
        P(("groups", "row", "col")),
    )
    return jax.shard_map(
        per_device,
        mesh=mesh,
        in_specs=placed,
        out_specs=P("groups", None, "row", "col"),
        check_vma=False,
    )
```

```python
import functools
import math

import jax
import jax.numpy as jnp
from jax import lax
from jax.experimental import pallas as pl
from jax.experimental.pallas import tpu as pltpu
from jax.sharding import PartitionSpec as P

NS = 3072
FREQ = 2
THIRDS = 3
BF16 = jnp.bfloat16
F32 = jnp.float32


def hop(pair, k, n_row):
    down = [(r, r - 1) for r in range(1, n_row) if r + k - 1 < n_row]
    up = [(r, r + 1) for r in range(n_row - 1) if r - k + 1 >= 0]
    return lax.ppermute(pair[0], "row", down), lax.ppermute(pair[1], "row", up)


CHEAP = pl.CostEstimate(flops=1000, bytes_accessed=1000, transcendentals=0)


def bin_kernel(picker, data, out):
    n_row, cap = out.shape[0], out.shape[2]
    cols = data.shape[2]
    for p in range(2):
        rows = jnp.dot(picker[...], data[p], preferred_element_type=F32).astype(BF16)
        for b in range(n_row):
            out[b, 0, :, p * cols : (p + 1) * cols] = rows[b * cap : (b + 1) * cap]


def bin_rows(picker, data, f, n_row, n_col):
    planes, own_cap, order = data.shape
    cap = picker.shape[0] // n_row
    cols = order // n_col
    return pl.pallas_call(
        bin_kernel,
        grid=(n_col,),
        in_specs=[
            pl.BlockSpec(picker.shape, lambda c: (0, 0)),
            pl.BlockSpec((2, own_cap, cols), lambda c: (f, 0, c)),
        ],
        out_specs=pl.BlockSpec((n_row, 1, cap, 2 * cols), lambda c: (0, c, 0, 0)),
        out_shape=jax.ShapeDtypeStruct((n_row, n_col, cap, 2 * cols), BF16),
        compiler_params=pltpu.CompilerParams(vmem_limit_bytes=24 * 2**20),
        cost_estimate=CHEAP,
    )(picker, data)


def place_kernel(placer, got, tile, *parts):
    rows = jnp.dot(placer[...], got[...], preferred_element_type=F32).astype(BF16)
    tile[0] = rows
    at = 0
    for part in parts:
        part[0] = rows[:, at : at + part.shape[2]]
        at += part.shape[2]


def place_rows(placer, got, parts):
    block_rows, arrived = placer.shape
    cols = got.shape[1] // 2
    sizes = [cols] + [n * cols // THIRDS for n in parts]
    return pl.pallas_call(
        place_kernel,
        grid=(2,),
        in_specs=[
            pl.BlockSpec(placer.shape, lambda p: (0, 0)),
            pl.BlockSpec((arrived, cols), lambda p: (0, p)),
        ],
        out_specs=[pl.BlockSpec((1, block_rows, n), lambda p: (p, 0, 0)) for n in sizes],
        out_shape=[jax.ShapeDtypeStruct((2, block_rows, n), BF16) for n in sizes],
        compiler_params=pltpu.CompilerParams(vmem_limit_bytes=32 * 2**20),
        cost_estimate=CHEAP,
    )(placer, got)


def after(value, earlier):
    return lax.optimization_barrier((value, earlier))[0]


def gather_cols(piece, n_col, second_after=None):
    held = {0: piece}
    bit = n_col // 2
    while bit:
        if second_after is not None and len(held) == 2:
            held = {d: after(a, second_after) for d, a in held.items()}
        pairs = [(c, c ^ bit) for c in range(n_col)]
        arrived = {d ^ bit: lax.ppermute(a, "col", pairs) for d, a in held.items()}
        held.update(arrived)
        bit //= 2
    return [held[d] for d in range(n_col)]


def product_kernel(opts, where, *refs):
    views, groups, order, n_col = (opts[k] for k in ("views", "groups", "order", "n_col"))
    by_xor, count = opts["by_xor"], len(views)
    arrays, refs = refs[: opts["lefts"]], refs[opts["lefts"] :]
    sources, refs = refs[: opts["sources"]], refs[opts["sources"] :]
    before = refs[0] if opts["before"] else None
    *outs, left, right, total, left_sems, sems = refs[opts["before"] + opts["held"] :]
    row, me = where[0], where[1]
    sub = right.shape[2] // 2
    depth = right.shape[1] // n_col
    first = groups[0][0] * sub
    step, third = pl.program_id(0), pl.program_id(1)

    def left_copies(c):
        found, at = [], 0
        for g, group in enumerate(groups):
            source = arrays[g * n_col + c] if by_xor else arrays[g].at[c]
            lanes = pl.ds(at, len(group) * sub)
            found.append(pltpu.make_async_copy(source, left.at[c, :, :, lanes], left_sems.at[g, c]))
            at += len(group) * sub
        return found

    def right_copies(t, s, lane, c):
        block = me ^ c if by_xor else c
        start = pl.multiple_of(block * depth, 32) if by_xor else block * depth
        found = []
        for p in range(2):
            source, lanes = sources[s], pl.ds(lane, sub)
            if len(source.shape) == 4:
                rows = source.at[block, p, pl.ds(first, depth), lanes]
            elif source.shape[1] == NS:
                rows = source.at[p, pl.ds(pl.multiple_of(block * sub * THIRDS + first, 32), depth), lanes]
            else:
                rows = source.at[p, pl.ds(first, depth), lanes]
            target = right.at[t, pl.ds(start, depth), pl.ds(p * sub, sub)]
            found.append(pltpu.make_async_copy(rows, target, sems.at[t, p, c]))
        return found

    def start_all(c):
        for copy in left_copies(c):
            copy.start()
        for t, (found, lane) in enumerate(views):
            for s, up in found:
                if up is None:
                    for copy in right_copies(t, s, lane, c):
                        copy.start()
                    continue

                @pl.when(row + up == (me ^ c if by_xor else c))
                def _(t=t, s=s, lane=lane):
                    for copy in right_copies(t, s, lane, c):
                        copy.start()

    for c in range(n_col):

        @pl.when((third == 0) & (step == c))
        def _(c=c):
            if c == 0:
                start_all(0)
            if c + 1 < n_col:
                start_all(c + 1)
            for copy in left_copies(c):
                copy.wait()

        for t, (found, lane) in enumerate(views):

            @pl.when((third == t) & (step == c))
            def _(c=c, t=t, s=found[0][0], lane=lane):
                for copy in right_copies(t, s, lane, c):
                    copy.wait()

    block = me ^ step if by_xor else step
    rows = right[third, pl.ds(pl.multiple_of(block * depth, 32), depth), :]
    by_real = jnp.dot(left[step, 0], rows, preferred_element_type=F32)
    by_imag = jnp.dot(left[step, 1], rows, preferred_element_type=F32)
    real = by_real[:, :sub] - by_imag[:, sub:]
    imag = by_real[:, sub:] + by_imag[:, :sub]

    @pl.when(step == 0)
    def _():
        total[third, 0] = real if before is None else real + before[0]
        total[third, 1] = imag if before is None else imag + before[1]

    @pl.when(step > 0)
    def _():
        total[third, 0] += real
        total[third, 1] += imag

    @pl.when(step == n_col - 1)
    def _():
        for p in range(2):
            if order is None:
                outs[0][p] = total[third, p]
                continue
            value = (total[third, p] * opts["weight"]).astype(BF16)
            outs[0][0, p] = value
            if len(outs) > 1:
                outs[1][p] = value


def complex_product(where, lefts, sources, views, shape, held, at, before=None):
    groups = [group for _, group in lefts]
    by_xor = isinstance(lefts[0][0], list)
    arrays = [a for pieces, _ in lefts for a in pieces] if by_xor else [a for a, _ in lefts]
    n_col = len(lefts[0][0]) if by_xor else arrays[0].shape[0]
    rows = arrays[0].shape[-2]
    sub = arrays[0].shape[-1] // len(groups[0])
    lanes = sum(len(g) for g in groups) * sub
    order, count = None, len(views)

    def late(c, t):
        return jnp.where(c == n_col - 1, t, 0)

    if at is None:
        out_specs = [pl.BlockSpec((2, rows, sub), lambda c, t, s: (0, 0, late(c, t)))]
        out_shape = [jax.ShapeDtypeStruct((2, rows, count * sub), F32)]
    else:
        order, f, third = at
        out_specs = [pl.BlockSpec((1, 2, rows, sub), lambda c, t, s: (order, f, 0, third + late(c, t)))]
        out_shape = [jax.ShapeDtypeStruct(shape, BF16)]
        if order == 0:
            out_specs.append(pl.BlockSpec((2, rows, sub), lambda c, t, s: (0, 0, late(c, t))))
            out_shape.append(jax.ShapeDtypeStruct((2, rows, count * sub), BF16))
    in_specs = [pl.BlockSpec(memory_space=pl.ANY)] * (len(arrays) + len(sources))
    args = [*arrays, *sources]
    if before is not None:
        in_specs.append(pl.BlockSpec((2, rows, sub), lambda c, t, s: (0, 0, jnp.where(c == 0, t, count - 1))))
        args.append(before)
    aliases = {1 + len(args) + k: k for k in range(len(held))}
    in_specs += [pl.BlockSpec(memory_space=pl.ANY)] * len(held)
    opts = dict(
        views=views,
        groups=groups,
        order=order,
        n_col=n_col,
        lefts=len(arrays),
        sources=len(sources),
        by_xor=by_xor,
        weight=1.0 / math.sqrt(2.0 * NS),
        before=int(before is not None),
        held=len(held),
    )
    return pl.pallas_call(
        functools.partial(product_kernel, opts),
        grid_spec=pltpu.PrefetchScalarGridSpec(
            num_scalar_prefetch=1,
            grid=(n_col, count),
            in_specs=in_specs,
            out_specs=out_specs,
            scratch_shapes=[
                pltpu.VMEM((n_col, 2, rows, lanes), BF16),
                pltpu.VMEM((count, lanes * n_col, 2 * sub), BF16),
                pltpu.VMEM((count, 2, rows, sub), F32),
                pltpu.SemaphoreType.DMA((len(groups), n_col)),
                pltpu.SemaphoreType.DMA((count, 2, n_col)),
            ],
        ),
        out_shape=out_shape,
        input_output_aliases=aliases,
        compiler_params=pltpu.CompilerParams(vmem_limit_bytes=(44 if count > 1 else 24) * 2**20),
        cost_estimate=CHEAP,
    )(where, *args, *held)


def per_device(acq_data, grid_row, counts):
    n_row = lax.axis_size("row")
    n_col = lax.axis_size("col")
    own_cap, planes, order = acq_data.shape
    block_rows = order // n_row
    tile_cols = order // n_col
    cap = own_cap // n_row
    slots = n_row * cap
    wide = 2 * tile_cols // THIRDS
    everything = tuple(range(THIRDS))

    slot_index = jnp.arange(own_cap, dtype=jnp.int32)
    block = jnp.where(slot_index < counts[0], grid_row // block_rows, n_row)
    earlier = (block[None, :] == block[:, None]) & (slot_index[None, :] < slot_index[:, None])
    rank = jnp.sum(earlier.astype(jnp.int32), axis=1)
    leaving = jnp.where(block < n_row, block * cap + rank, -1)
    hit = jnp.arange(slots, dtype=jnp.int32)[:, None] == leaving[None, :]
    spots = jnp.sum(jnp.where(hit, (grid_row % block_rows)[None, :] + 1, 0), axis=1) - 1
    picker = hit.astype(BF16)
    data = jnp.transpose(acq_data, (1, 0, 2))
    line = n_row <= 4 and block_rows == tile_cols
    my_row = lax.axis_index("row")
    labels = jnp.broadcast_to(spots.reshape(n_row, 1, cap), (n_row, n_col, cap))
    places = lax.all_to_all(
        labels.reshape(n_row * n_col, cap), ("row", "col"), split_axis=0, concat_axis=0, tiled=True
    ).reshape(-1)
    placer = (jnp.arange(block_rows, dtype=jnp.int32)[:, None] == places[None, :]).astype(BF16)

    tiles, lefts = [], []
    pair = None
    for f in range(FREQ):
        sent = bin_rows(picker, data, f, n_row, n_col)
        if f == 0:
            sent = after(sent, places)
        got = lax.all_to_all(
            sent.reshape(n_row * n_col, cap, 2 * tile_cols), ("row", "col"), split_axis=0, concat_axis=0, tiled=True
        ).reshape(-1, 2 * tile_cols)
        if pair is not None:
            got, pair, _ = lax.optimization_barrier((got, pair, lefts[0][0]))
        tile, *cut = place_rows(placer, got, (THIRDS - 1, 1) if f else ())
        if line and f == 0:
            pair = hop((tile, tile), 1, n_row)
        tiles.append(tile)
        lefts.append((lax.all_gather(tile, "col", axis=0), everything))

    def gather_rows(part):
        if block_rows == tile_cols:
            return lax.all_gather(part, "row", axis=0)
        return lax.all_gather(part, "row", axis=1, tiled=True)

    sub = tile_cols // THIRDS
    right1 = [gather_rows(after(part, lefts[1][0])) for part in cut]
    views1 = [([(0, None)], j * sub) for j in everything[:-1]] + [([(1, None)], 0)]
    if line:
        right0, ups = [tiles[0], *pair], [0, 1, -1]
        for k in range(2, n_row):
            pair = hop(pair, k, n_row)
            right0 += list(pair)
            ups += [k, -k]
        right0[0] = after(right0[0], lefts[1][0])
    else:
        right0, ups = [gather_rows(tiles[0])], [None]
    views0 = [(list(enumerate(ups)), j * sub) for j in everything]

    where = jnp.stack([my_row, lax.axis_index("col")]).astype(jnp.int32)
    product = functools.partial(complex_product, where)
    shape = (2, planes, block_rows, tile_cols)
    result, piece = product([lefts[0]], right0, views0, shape, (), (0, 0, 0))
    found = gather_cols(piece, n_col)
    found[0], right1[0] = lax.optimization_barrier((found[0], right1[0]))
    (result,) = product([(found, everything)], right0, views0, shape, (result,), (1, 0, 0))
    result, piece = product([lefts[1]], right1[:1], views1[:-1], shape, (result,), (0, 1, 0))
    most = (gather_cols(piece, n_col), everything[:-1])
    result, piece = product([lefts[1]], right1[1:], [([(0, None)], 0)], shape, (result,), (0, 1, THIRDS - 1))
    rest = (gather_cols(piece, n_col), everything[-1:])
    (sums,) = product([most], right1, views1, shape, (), None)
    return product([rest], right1, views1, shape, (result,), (1, 1, 0), before=sums)[0]


def solution(mesh):
    placed = (
        P(("groups", "row", "col"), None, None),
        P(("groups", "row", "col")),
        P(("groups", "row", "col")),
    )
    return jax.shard_map(
        per_device,
        mesh=mesh,
        in_specs=placed,
        out_specs=P("groups", None, "row", "col"),
        check_vma=False,
    )
```

```python
import functools
import math

import jax
import jax.numpy as jnp
from jax import lax
from jax.experimental import pallas as pl
from jax.experimental.pallas import tpu as pltpu
from jax.sharding import PartitionSpec as P

NS = 3072
FREQ = 2
THIRDS = 3
BF16 = jnp.bfloat16
F32 = jnp.float32


def hop(pair, k, n_row):
    down = [(r, r - 1) for r in range(1, n_row) if r + k - 1 < n_row]
    up = [(r, r + 1) for r in range(n_row - 1) if r - k + 1 >= 0]
    return lax.ppermute(pair[0], "row", down), lax.ppermute(pair[1], "row", up)


CHEAP = pl.CostEstimate(flops=1000, bytes_accessed=1000, transcendentals=0)


def bin_kernel(picker, data, out):
    n_row, cap = out.shape[0], out.shape[2]
    cols = data.shape[2]
    for p in range(2):
        rows = jnp.dot(picker[...], data[p], preferred_element_type=F32).astype(BF16)
        for b in range(n_row):
            out[b, 0, :, p * cols : (p + 1) * cols] = rows[b * cap : (b + 1) * cap]


def bin_rows(picker, data, f, n_row, n_col):
    planes, own_cap, order = data.shape
    cap = picker.shape[0] // n_row
    cols = order // n_col
    return pl.pallas_call(
        bin_kernel,
        grid=(n_col,),
        in_specs=[
            pl.BlockSpec(picker.shape, lambda c: (0, 0)),
            pl.BlockSpec((2, own_cap, cols), lambda c: (f, 0, c)),
        ],
        out_specs=pl.BlockSpec((n_row, 1, cap, 2 * cols), lambda c: (0, c, 0, 0)),
        out_shape=jax.ShapeDtypeStruct((n_row, n_col, cap, 2 * cols), BF16),
        compiler_params=pltpu.CompilerParams(vmem_limit_bytes=24 * 2**20),
        cost_estimate=CHEAP,
    )(picker, data)


def place_kernel(placer, got, tile, *parts):
    rows = jnp.dot(placer[...], got[...], preferred_element_type=F32).astype(BF16)
    tile[0] = rows
    at = 0
    for part in parts:
        part[0] = rows[:, at : at + part.shape[2]]
        at += part.shape[2]


def place_rows(placer, got, parts):
    block_rows, arrived = placer.shape
    cols = got.shape[1] // 2
    sizes = [cols] + [n * cols // THIRDS for n in parts]
    return pl.pallas_call(
        place_kernel,
        grid=(2,),
        in_specs=[
            pl.BlockSpec(placer.shape, lambda p: (0, 0)),
            pl.BlockSpec((arrived, cols), lambda p: (0, p)),
        ],
        out_specs=[pl.BlockSpec((1, block_rows, n), lambda p: (p, 0, 0)) for n in sizes],
        out_shape=[jax.ShapeDtypeStruct((2, block_rows, n), BF16) for n in sizes],
        compiler_params=pltpu.CompilerParams(vmem_limit_bytes=32 * 2**20),
        cost_estimate=CHEAP,
    )(placer, got)


def after(value, earlier):
    return lax.optimization_barrier((value, earlier))[0]


def gather_cols(piece, n_col, second_after=None):
    held = {0: piece}
    bit = n_col // 2
    while bit:
        if second_after is not None and len(held) == 2:
            held = {d: after(a, second_after) for d, a in held.items()}
        pairs = [(c, c ^ bit) for c in range(n_col)]
        arrived = {d ^ bit: lax.ppermute(a, "col", pairs) for d, a in held.items()}
        held.update(arrived)
        bit //= 2
    return [held[d] for d in range(n_col)]


def product_kernel(opts, where, *refs):
    views, groups, order, n_col = (opts[k] for k in ("views", "groups", "order", "n_col"))
    by_xor, count = opts["by_xor"], len(views)
    arrays, refs = refs[: opts["lefts"]], refs[opts["lefts"] :]
    sources, refs = refs[: opts["sources"]], refs[opts["sources"] :]
    before = refs[0] if opts["before"] else None
    *outs, left, right, total, left_sems, sems = refs[opts["before"] + opts["held"] :]
    row, me = where[0], where[1]
    sub = right.shape[2] // 2
    depth = right.shape[1] // n_col
    first = groups[0][0] * sub
    step, third = pl.program_id(0), pl.program_id(1)

    def left_copies(c):
        found, at = [], 0
        for g, group in enumerate(groups):
            source = arrays[g * n_col + c] if by_xor else arrays[g].at[c]
            lanes = pl.ds(at, len(group) * sub)
            found.append(pltpu.make_async_copy(source, left.at[c, :, :, lanes], left_sems.at[g, c]))
            at += len(group) * sub
        return found

    def right_copies(t, s, lane, c):
        block = me ^ c if by_xor else c
        start = pl.multiple_of(block * depth, 32) if by_xor else block * depth
        found = []
        for p in range(2):
            source, lanes = sources[s], pl.ds(lane, sub)
            if len(source.shape) == 4:
                rows = source.at[block, p, pl.ds(first, depth), lanes]
            elif source.shape[1] == NS:
                rows = source.at[p, pl.ds(pl.multiple_of(block * sub * THIRDS + first, 32), depth), lanes]
            else:
                rows = source.at[p, pl.ds(first, depth), lanes]
            target = right.at[t, pl.ds(start, depth), pl.ds(p * sub, sub)]
            found.append(pltpu.make_async_copy(rows, target, sems.at[t, p, c]))
        return found

    def start_all(c):
        for copy in left_copies(c):
            copy.start()
        for t, (found, lane) in enumerate(views):
            for s, up in found:
                if up is None:
                    for copy in right_copies(t, s, lane, c):
                        copy.start()
                    continue

                @pl.when(row + up == (me ^ c if by_xor else c))
                def _(t=t, s=s, lane=lane):
                    for copy in right_copies(t, s, lane, c):
                        copy.start()

    for c in range(n_col):

        @pl.when((third == 0) & (step == c))
        def _(c=c):
            if c == 0:
                start_all(0)
            if c + 1 < n_col:
                start_all(c + 1)
            for copy in left_copies(c):
                copy.wait()

        for t, (found, lane) in enumerate(views):

            @pl.when((third == t) & (step == c))
            def _(c=c, t=t, s=found[0][0], lane=lane):
                for copy in right_copies(t, s, lane, c):
                    copy.wait()

    block = me ^ step if by_xor else step
    rows = right[third, pl.ds(pl.multiple_of(block * depth, 32), depth), :]

    @pl.when(step == 0)
    def _():
        for p in range(2):
            total[third, p] = jnp.dot(left[step, p], rows, preferred_element_type=F32)

    @pl.when(step > 0)
    def _():
        for p in range(2):
            total[third, p] += jnp.dot(left[step, p], rows, preferred_element_type=F32)

    @pl.when(step == n_col - 1)
    def _():
        real = total[third, 0, :, :sub] - total[third, 1, :, sub:]
        imag = total[third, 0, :, sub:] + total[third, 1, :, :sub]
        for p, value in enumerate((real, imag)):
            if before is not None:
                value = value + before[p]
            if order is None:
                outs[0][p] = value
                continue
            value = (value * opts["weight"]).astype(BF16)
            outs[0][0, p] = value
            if len(outs) > 1:
                outs[1][p] = value


def complex_product(where, lefts, sources, views, shape, held, at, before=None):
    groups = [group for _, group in lefts]
    by_xor = isinstance(lefts[0][0], list)
    arrays = [a for pieces, _ in lefts for a in pieces] if by_xor else [a for a, _ in lefts]
    n_col = len(lefts[0][0]) if by_xor else arrays[0].shape[0]
    rows = arrays[0].shape[-2]
    sub = arrays[0].shape[-1] // len(groups[0])
    lanes = sum(len(g) for g in groups) * sub
    order, count = None, len(views)

    def late(c, t):
        return jnp.where(c == n_col - 1, t, 0)

    if at is None:
        out_specs = [pl.BlockSpec((2, rows, sub), lambda c, t, s: (0, 0, late(c, t)))]
        out_shape = [jax.ShapeDtypeStruct((2, rows, count * sub), F32)]
    else:
        order, f, third = at
        out_specs = [pl.BlockSpec((1, 2, rows, sub), lambda c, t, s: (order, f, 0, third + late(c, t)))]
        out_shape = [jax.ShapeDtypeStruct(shape, BF16)]
        if order == 0:
            out_specs.append(pl.BlockSpec((2, rows, sub), lambda c, t, s: (0, 0, late(c, t))))
            out_shape.append(jax.ShapeDtypeStruct((2, rows, count * sub), BF16))
    in_specs = [pl.BlockSpec(memory_space=pl.ANY)] * (len(arrays) + len(sources))
    args = [*arrays, *sources]
    if before is not None:
        in_specs.append(pl.BlockSpec((2, rows, sub), lambda c, t, s: (0, 0, late(c, t))))
        args.append(before)
    aliases = {1 + len(args) + k: k for k in range(len(held))}
    in_specs += [pl.BlockSpec(memory_space=pl.ANY)] * len(held)
    opts = dict(
        views=views,
        groups=groups,
        order=order,
        n_col=n_col,
        lefts=len(arrays),
        sources=len(sources),
        by_xor=by_xor,
        weight=1.0 / math.sqrt(2.0 * NS),
        before=int(before is not None),
        held=len(held),
    )
    return pl.pallas_call(
        functools.partial(product_kernel, opts),
        grid_spec=pltpu.PrefetchScalarGridSpec(
            num_scalar_prefetch=1,
            grid=(n_col, count),
            in_specs=in_specs,
            out_specs=out_specs,
            scratch_shapes=[
                pltpu.VMEM((n_col, 2, rows, lanes), BF16),
                pltpu.VMEM((count, lanes * n_col, 2 * sub), BF16),
                pltpu.VMEM((count, 2, rows, 2 * sub), F32),
                pltpu.SemaphoreType.DMA((len(groups), n_col)),
                pltpu.SemaphoreType.DMA((count, 2, n_col)),
            ],
        ),
        out_shape=out_shape,
        input_output_aliases=aliases,
        compiler_params=pltpu.CompilerParams(vmem_limit_bytes=(44 if count > 1 else 24) * 2**20),
        cost_estimate=CHEAP,
    )(where, *args, *held)


def per_device(acq_data, grid_row, counts):
    n_row = lax.axis_size("row")
    n_col = lax.axis_size("col")
    own_cap, planes, order = acq_data.shape
    block_rows = order // n_row
    tile_cols = order // n_col
    cap = own_cap // n_row
    slots = n_row * cap
    wide = 2 * tile_cols // THIRDS
    everything = tuple(range(THIRDS))

    slot_index = jnp.arange(own_cap, dtype=jnp.int32)
    block = jnp.where(slot_index < counts[0], grid_row // block_rows, n_row)
    earlier = (block[None, :] == block[:, None]) & (slot_index[None, :] < slot_index[:, None])
    rank = jnp.sum(earlier.astype(jnp.int32), axis=1)
    leaving = jnp.where(block < n_row, block * cap + rank, -1)
    hit = jnp.arange(slots, dtype=jnp.int32)[:, None] == leaving[None, :]
    spots = jnp.sum(jnp.where(hit, (grid_row % block_rows)[None, :] + 1, 0), axis=1) - 1
    picker = hit.astype(BF16)
    data = jnp.transpose(acq_data, (1, 0, 2))
    line = n_row <= 4 and block_rows == tile_cols
    my_row = lax.axis_index("row")
    labels = jnp.broadcast_to(spots.reshape(n_row, 1, cap), (n_row, n_col, cap))
    places = lax.all_to_all(
        labels.reshape(n_row * n_col, cap), ("row", "col"), split_axis=0, concat_axis=0, tiled=True
    ).reshape(-1)
    placer = (jnp.arange(block_rows, dtype=jnp.int32)[:, None] == places[None, :]).astype(BF16)

    tiles, lefts = [], []
    pair = None
    for f in range(FREQ):
        sent = bin_rows(picker, data, f, n_row, n_col)
        if f == 0:
            sent = after(sent, places)
        got = lax.all_to_all(
            sent.reshape(n_row * n_col, cap, 2 * tile_cols), ("row", "col"), split_axis=0, concat_axis=0, tiled=True
        ).reshape(-1, 2 * tile_cols)
        if pair is not None:
            got, pair, _ = lax.optimization_barrier((got, pair, lefts[0][0]))
        tile, *cut = place_rows(placer, got, (THIRDS - 1, 1) if f else ())
        if line and f == 0:
            pair = hop((tile, tile), 1, n_row)
        tiles.append(tile)
        if f == 0:
            lefts.append((lax.all_gather(tile, "col", axis=0), everything))

    def gather_rows(part):
        if block_rows == tile_cols:
            return lax.all_gather(part, "row", axis=0)
        return lax.all_gather(part, "row", axis=1, tiled=True)

    sub = tile_cols // THIRDS
    views1 = [([(0, None)], j * sub) for j in everything[:-1]] + [([(1, None)], 0)]
    second = None
    if line:
        right0, ups = [tiles[0], *pair], [0, 1, -1]
        for k in range(2, n_row):
            pair = hop(pair, k, n_row)
            second = pair if k == 2 else second
            right0 += list(pair)
            ups += [k, -k]
        cut = [after(part, second) for part in cut]
    else:
        right0, ups = [gather_rows(tiles[0])], [None]
    right1 = [gather_rows(part) for part in cut]
    lefts.append((gather_cols(tiles[1], n_col, second), everything))
    right0[0] = after(right0[0], lefts[1][0])
    views0 = [(list(enumerate(ups)), j * sub) for j in everything]

    where = jnp.stack([my_row, lax.axis_index("col")]).astype(jnp.int32)
    product = functools.partial(complex_product, where)
    shape = (2, planes, block_rows, tile_cols)
    result, piece = product([lefts[0]], right0, views0, shape, (), (0, 0, 0))
    found = gather_cols(piece, n_col)
    (result,) = product([(found, everything)], right0, views0, shape, (result,), (1, 0, 0))
    result, piece = product([lefts[1]], right1[:1], views1[:-1], shape, (result,), (0, 1, 0))
    most = (gather_cols(piece, n_col), everything[:-1])
    result, piece = product([lefts[1]], right1[1:], [([(0, None)], 0)], shape, (result,), (0, 1, THIRDS - 1))
    rest = (gather_cols(piece, n_col), everything[-1:])
    (sums,) = product([most], right1, views1, shape, (), None)
    return product([rest], right1, views1, shape, (result,), (1, 1, 0), before=sums)[0]


def solution(mesh):
    placed = (
        P(("groups", "row", "col"), None, None),
        P(("groups", "row", "col")),
        P(("groups", "row", "col")),
    )
    return jax.shard_map(
        per_device,
        mesh=mesh,
        in_specs=placed,
        out_specs=P("groups", None, "row", "col"),
        check_vma=False,
    )
```

```python
import functools
import math

import jax
import jax.numpy as jnp
from jax import lax
from jax.experimental import pallas as pl
from jax.experimental.pallas import tpu as pltpu
from jax.sharding import PartitionSpec as P

NS = 3072
FREQ = 2
THIRDS = 3
BF16 = jnp.bfloat16
F32 = jnp.float32


def hop(pair, k, n_row):
    down = [(r, r - 1) for r in range(1, n_row) if r + k - 1 < n_row]
    up = [(r, r + 1) for r in range(n_row - 1) if r - k + 1 >= 0]
    return lax.ppermute(pair[0], "row", down), lax.ppermute(pair[1], "row", up)


CHEAP = pl.CostEstimate(flops=1000, bytes_accessed=1000, transcendentals=0)


def bin_kernel(picker, data, out):
    n_row, cap = out.shape[0], out.shape[2]
    cols = data.shape[2]
    for p in range(2):
        rows = jnp.dot(picker[...], data[p], preferred_element_type=F32).astype(BF16)
        for b in range(n_row):
            out[b, 0, :, p * cols : (p + 1) * cols] = rows[b * cap : (b + 1) * cap]


def bin_rows(picker, data, f, n_row, n_col):
    planes, own_cap, order = data.shape
    cap = picker.shape[0] // n_row
    cols = order // n_col
    return pl.pallas_call(
        bin_kernel,
        grid=(n_col,),
        in_specs=[
            pl.BlockSpec(picker.shape, lambda c: (0, 0)),
            pl.BlockSpec((2, own_cap, cols), lambda c: (f, 0, c)),
        ],
        out_specs=pl.BlockSpec((n_row, 1, cap, 2 * cols), lambda c: (0, c, 0, 0)),
        out_shape=jax.ShapeDtypeStruct((n_row, n_col, cap, 2 * cols), BF16),
        compiler_params=pltpu.CompilerParams(vmem_limit_bytes=24 * 2**20),
        cost_estimate=CHEAP,
    )(picker, data)


def place_kernel(placer, got, tile, *parts):
    rows = jnp.dot(placer[...], got[...], preferred_element_type=F32).astype(BF16)
    tile[0] = rows
    at = 0
    for part in parts:
        part[0] = rows[:, at : at + part.shape[2]]
        at += part.shape[2]


def place_rows(placer, got, parts):
    block_rows, arrived = placer.shape
    cols = got.shape[1] // 2
    sizes = [cols] + [n * cols // THIRDS for n in parts]
    return pl.pallas_call(
        place_kernel,
        grid=(2,),
        in_specs=[
            pl.BlockSpec(placer.shape, lambda p: (0, 0)),
            pl.BlockSpec((arrived, cols), lambda p: (0, p)),
        ],
        out_specs=[pl.BlockSpec((1, block_rows, n), lambda p: (p, 0, 0)) for n in sizes],
        out_shape=[jax.ShapeDtypeStruct((2, block_rows, n), BF16) for n in sizes],
        compiler_params=pltpu.CompilerParams(vmem_limit_bytes=32 * 2**20),
        cost_estimate=CHEAP,
    )(placer, got)


def after(value, earlier):
    return lax.optimization_barrier((value, earlier))[0]


def gather_cols(piece, n_col, second_after=None):
    held = {0: piece}
    bit = n_col // 2
    while bit:
        if second_after is not None and len(held) == 2:
            held = {d: after(a, second_after) for d, a in held.items()}
        pairs = [(c, c ^ bit) for c in range(n_col)]
        arrived = {d ^ bit: lax.ppermute(a, "col", pairs) for d, a in held.items()}
        held.update(arrived)
        bit //= 2
    return [held[d] for d in range(n_col)]


def product_kernel(opts, where, *refs):
    views, groups, order, n_col = (opts[k] for k in ("views", "groups", "order", "n_col"))
    by_xor, count = opts["by_xor"], len(views)
    arrays, refs = refs[: opts["lefts"]], refs[opts["lefts"] :]
    sources, refs = refs[: opts["sources"]], refs[opts["sources"] :]
    before = refs[0] if opts["before"] else None
    *outs, left, right, total, left_sems, sems = refs[opts["before"] + opts["held"] :]
    row, me = where[0], where[1]
    sub = right.shape[2] // 2
    depth = right.shape[1] // n_col
    first = groups[0][0] * sub
    step, third = pl.program_id(0), pl.program_id(1)

    def left_copies(c):
        found, at = [], 0
        for g, group in enumerate(groups):
            source = arrays[g * n_col + c] if by_xor else arrays[g].at[c]
            lanes = pl.ds(at, len(group) * sub)
            found.append(pltpu.make_async_copy(source, left.at[c, :, :, lanes], left_sems.at[g, c]))
            at += len(group) * sub
        return found

    def right_copies(t, s, lane, c):
        block = me ^ c if by_xor else c
        start = pl.multiple_of(block * depth, 32) if by_xor else block * depth
        found = []
        for p in range(2):
            source, lanes = sources[s], pl.ds(lane, sub)
            if len(source.shape) == 4:
                rows = source.at[block, p, pl.ds(first, depth), lanes]
            elif source.shape[1] == NS:
                rows = source.at[p, pl.ds(pl.multiple_of(block * sub * THIRDS + first, 32), depth), lanes]
            else:
                rows = source.at[p, pl.ds(first, depth), lanes]
            target = right.at[t, pl.ds(start, depth), pl.ds(p * sub, sub)]
            found.append(pltpu.make_async_copy(rows, target, sems.at[t, p, c]))
        return found

    def start_all(c):
        for copy in left_copies(c):
            copy.start()
        for t, (found, lane) in enumerate(views):
            for s, up in found:
                if up is None:
                    for copy in right_copies(t, s, lane, c):
                        copy.start()
                    continue

                @pl.when(row + up == (me ^ c if by_xor else c))
                def _(t=t, s=s, lane=lane):
                    for copy in right_copies(t, s, lane, c):
                        copy.start()

    for c in range(n_col):

        @pl.when((third == 0) & (step == c))
        def _(c=c):
            if c == 0:
                start_all(0)
            if c + 1 < n_col:
                start_all(c + 1)
            for copy in left_copies(c):
                copy.wait()

        for t, (found, lane) in enumerate(views):

            @pl.when((third == t) & (step == c))
            def _(c=c, t=t, s=found[0][0], lane=lane):
                for copy in right_copies(t, s, lane, c):
                    copy.wait()

    block = me ^ step if by_xor else step
    rows = right[third, pl.ds(pl.multiple_of(block * depth, 32), depth), :]

    @pl.when(step == 0)
    def _():
        for p in range(2):
            total[third, p] = jnp.dot(left[step, p], rows, preferred_element_type=F32)

    @pl.when(step > 0)
    def _():
        for p in range(2):
            total[third, p] += jnp.dot(left[step, p], rows, preferred_element_type=F32)

    @pl.when(step == n_col - 1)
    def _():
        real = total[third, 0, :, :sub] - total[third, 1, :, sub:]
        imag = total[third, 0, :, sub:] + total[third, 1, :, :sub]
        for p, value in enumerate((real, imag)):
            if before is not None:
                value = value + before[p]
            if order is None:
                outs[0][p] = value
                continue
            value = (value * opts["weight"]).astype(BF16)
            outs[0][0, p] = value
            if len(outs) > 1:
                outs[1][p] = value


def complex_product(where, lefts, sources, views, shape, held, at, before=None):
    groups = [group for _, group in lefts]
    by_xor = isinstance(lefts[0][0], list)
    arrays = [a for pieces, _ in lefts for a in pieces] if by_xor else [a for a, _ in lefts]
    n_col = len(lefts[0][0]) if by_xor else arrays[0].shape[0]
    rows = arrays[0].shape[-2]
    sub = arrays[0].shape[-1] // len(groups[0])
    lanes = sum(len(g) for g in groups) * sub
    order, count = None, len(views)

    def late(c, t):
        return jnp.where(c == n_col - 1, t, 0)

    if at is None:
        out_specs = [pl.BlockSpec((2, rows, sub), lambda c, t, s: (0, 0, late(c, t)))]
        out_shape = [jax.ShapeDtypeStruct((2, rows, count * sub), F32)]
    else:
        order, f, third = at
        out_specs = [pl.BlockSpec((1, 2, rows, sub), lambda c, t, s: (order, f, 0, third + late(c, t)))]
        out_shape = [jax.ShapeDtypeStruct(shape, BF16)]
        if order == 0:
            out_specs.append(pl.BlockSpec((2, rows, sub), lambda c, t, s: (0, 0, late(c, t))))
            out_shape.append(jax.ShapeDtypeStruct((2, rows, count * sub), BF16))
    in_specs = [pl.BlockSpec(memory_space=pl.ANY)] * (len(arrays) + len(sources))
    args = [*arrays, *sources]
    if before is not None:
        in_specs.append(pl.BlockSpec((2, rows, sub), lambda c, t, s: (0, 0, late(c, t))))
        args.append(before)
    aliases = {1 + len(args) + k: k for k in range(len(held))}
    in_specs += [pl.BlockSpec(memory_space=pl.ANY)] * len(held)
    opts = dict(
        views=views,
        groups=groups,
        order=order,
        n_col=n_col,
        lefts=len(arrays),
        sources=len(sources),
        by_xor=by_xor,
        weight=1.0 / math.sqrt(2.0 * NS),
        before=int(before is not None),
        held=len(held),
    )
    return pl.pallas_call(
        functools.partial(product_kernel, opts),
        grid_spec=pltpu.PrefetchScalarGridSpec(
            num_scalar_prefetch=1,
            grid=(n_col, count),
            in_specs=in_specs,
            out_specs=out_specs,
            scratch_shapes=[
                pltpu.VMEM((n_col, 2, rows, lanes), BF16),
                pltpu.VMEM((count, lanes * n_col, 2 * sub), BF16),
                pltpu.VMEM((count, 2, rows, 2 * sub), F32),
                pltpu.SemaphoreType.DMA((len(groups), n_col)),
                pltpu.SemaphoreType.DMA((count, 2, n_col)),
            ],
        ),
        out_shape=out_shape,
        input_output_aliases=aliases,
        compiler_params=pltpu.CompilerParams(vmem_limit_bytes=(44 if count > 1 else 24) * 2**20),
        cost_estimate=CHEAP,
    )(where, *args, *held)


def per_device(acq_data, grid_row, counts):
    n_row = lax.axis_size("row")
    n_col = lax.axis_size("col")
    own_cap, planes, order = acq_data.shape
    block_rows = order // n_row
    tile_cols = order // n_col
    cap = own_cap // n_row
    slots = n_row * cap
    wide = 2 * tile_cols // THIRDS
    everything = tuple(range(THIRDS))

    slot_index = jnp.arange(own_cap, dtype=jnp.int32)
    block = jnp.where(slot_index < counts[0], grid_row // block_rows, n_row)
    earlier = (block[None, :] == block[:, None]) & (slot_index[None, :] < slot_index[:, None])
    rank = jnp.sum(earlier.astype(jnp.int32), axis=1)
    leaving = jnp.where(block < n_row, block * cap + rank, -1)
    hit = jnp.arange(slots, dtype=jnp.int32)[:, None] == leaving[None, :]
    spots = jnp.sum(jnp.where(hit, (grid_row % block_rows)[None, :] + 1, 0), axis=1) - 1
    picker = hit.astype(BF16)
    data = jnp.transpose(acq_data, (1, 0, 2))
    line = n_row <= 4 and block_rows == tile_cols
    my_row = lax.axis_index("row")
    labels = jnp.broadcast_to(spots.reshape(n_row, 1, cap), (n_row, n_col, cap))
    places = lax.all_to_all(
        labels.reshape(n_row * n_col, cap), ("row", "col"), split_axis=0, concat_axis=0, tiled=True
    ).reshape(-1)
    placer = (jnp.arange(block_rows, dtype=jnp.int32)[:, None] == places[None, :]).astype(BF16)

    tiles, lefts = [], []
    pair = None
    for f in range(FREQ):
        sent = bin_rows(picker, data, f, n_row, n_col)
        if f == 0:
            sent = after(sent, places)
        got = lax.all_to_all(
            sent.reshape(n_row * n_col, cap, 2 * tile_cols), ("row", "col"), split_axis=0, concat_axis=0, tiled=True
        ).reshape(-1, 2 * tile_cols)
        if pair is not None:
            got, pair, _ = lax.optimization_barrier((got, pair, lefts[0][0]))
        tile, *cut = place_rows(placer, got, (THIRDS - 1, 1) if f else ())
        if line and f == 0:
            pair = hop((tile, tile), 1, n_row)
        tiles.append(tile)
        if f == 0:
            lefts.append((lax.all_gather(tile, "col", axis=0), everything))

    def gather_rows(part):
        if block_rows == tile_cols:
            return lax.all_gather(part, "row", axis=0)
        return lax.all_gather(part, "row", axis=1, tiled=True)

    sub = tile_cols // THIRDS
    views1 = [([(0, None)], j * sub) for j in everything[:-1]] + [([(1, None)], 0)]
    second = None
    if line:
        right0, ups = [tiles[0], *pair], [0, 1, -1]
        for k in range(2, n_row):
            pair = hop(pair, k, n_row)
            second = pair if k == 2 else second
            right0 += list(pair)
            ups += [k, -k]
        cut = [after(part, second) for part in cut]
    else:
        right0, ups = [gather_rows(tiles[0])], [None]
    right1 = [gather_rows(part) for part in cut]
    lefts.append((gather_cols(tiles[1], n_col, pair), everything))
    views0 = [(list(enumerate(ups)), j * sub) for j in everything]

    where = jnp.stack([my_row, lax.axis_index("col")]).astype(jnp.int32)
    product = functools.partial(complex_product, where)
    shape = (2, planes, block_rows, tile_cols)
    result, piece = product([lefts[0]], right0, views0, shape, (), (0, 0, 0))
    found = gather_cols(piece, n_col)
    result, most = product([lefts[1]], right1[:1], views1[:-1], shape, (result,), (0, 1, 0))
    most = gather_cols(most, n_col)
    found[0] = after(found[0], right1[1])
    (result,) = product([(found, everything)], right0, views0, shape, (result,), (1, 0, 0))
    result, rest = product([lefts[1]], right1[1:], [([(0, None)], 0)], shape, (result,), (0, 1, THIRDS - 1))
    (sums,) = product([(most, everything[:-1])], right1, views1, shape, (), None)
    rest = gather_cols(after(rest, most[n_col // 2]), n_col, sums)
    return product([(rest, everything[-1:])], right1, views1, shape, (result,), (1, 1, 0), before=sums)[0]


def solution(mesh):
    placed = (
        P(("groups", "row", "col"), None, None),
        P(("groups", "row", "col")),
        P(("groups", "row", "col")),
    )
    return jax.shard_map(
        per_device,
        mesh=mesh,
        in_specs=placed,
        out_specs=P("groups", None, "row", "col"),
        check_vma=False,
    )
```

```python
import functools
import math

import jax
import jax.numpy as jnp
from jax import lax
from jax.experimental import pallas as pl
from jax.experimental.pallas import tpu as pltpu
from jax.sharding import PartitionSpec as P

NS = 3072
FREQ = 2
THIRDS = 3
BF16 = jnp.bfloat16
F32 = jnp.float32


def hop(pair, k, n_row):
    down = [(r, r - 1) for r in range(1, n_row) if r + k - 1 < n_row]
    up = [(r, r + 1) for r in range(n_row - 1) if r - k + 1 >= 0]
    return lax.ppermute(pair[0], "row", down), lax.ppermute(pair[1], "row", up)


CHEAP = pl.CostEstimate(flops=1000, bytes_accessed=1000, transcendentals=0)


def bin_kernel(picker, data, out):
    n_row, cap = out.shape[0], out.shape[2]
    cols = data.shape[2]
    for p in range(2):
        rows = jnp.dot(picker[...], data[p], preferred_element_type=F32).astype(BF16)
        for b in range(n_row):
            out[b, 0, :, p * cols : (p + 1) * cols] = rows[b * cap : (b + 1) * cap]


def bin_rows(picker, data, f, n_row, n_col):
    planes, own_cap, order = data.shape
    cap = picker.shape[0] // n_row
    cols = order // n_col
    return pl.pallas_call(
        bin_kernel,
        grid=(n_col,),
        in_specs=[
            pl.BlockSpec(picker.shape, lambda c: (0, 0)),
            pl.BlockSpec((2, own_cap, cols), lambda c: (f, 0, c)),
        ],
        out_specs=pl.BlockSpec((n_row, 1, cap, 2 * cols), lambda c: (0, c, 0, 0)),
        out_shape=jax.ShapeDtypeStruct((n_row, n_col, cap, 2 * cols), BF16),
        compiler_params=pltpu.CompilerParams(vmem_limit_bytes=24 * 2**20),
        cost_estimate=CHEAP,
    )(picker, data)


def place_kernel(placer, got, tile, *parts):
    rows = jnp.dot(placer[...], got[...], preferred_element_type=F32).astype(BF16)
    tile[0] = rows
    at = 0
    for part in parts:
        part[0] = rows[:, at : at + part.shape[2]]
        at += part.shape[2]


def place_rows(placer, got, parts):
    block_rows, arrived = placer.shape
    cols = got.shape[1] // 2
    sizes = [cols] + [n * cols // THIRDS for n in parts]
    return pl.pallas_call(
        place_kernel,
        grid=(2,),
        in_specs=[
            pl.BlockSpec(placer.shape, lambda p: (0, 0)),
            pl.BlockSpec((arrived, cols), lambda p: (0, p)),
        ],
        out_specs=[pl.BlockSpec((1, block_rows, n), lambda p: (p, 0, 0)) for n in sizes],
        out_shape=[jax.ShapeDtypeStruct((2, block_rows, n), BF16) for n in sizes],
        compiler_params=pltpu.CompilerParams(vmem_limit_bytes=32 * 2**20),
        cost_estimate=CHEAP,
    )(placer, got)


def after(value, earlier):
    return lax.optimization_barrier((value, earlier))[0]


def gather_cols(piece, n_col, second_after=None):
    held = {0: piece}
    bit = n_col // 2
    while bit:
        if second_after is not None and len(held) == 2:
            held = {d: after(a, second_after) for d, a in held.items()}
        pairs = [(c, c ^ bit) for c in range(n_col)]
        arrived = {d ^ bit: lax.ppermute(a, "col", pairs) for d, a in held.items()}
        held.update(arrived)
        bit //= 2
    return [held[d] for d in range(n_col)]


def product_kernel(opts, where, *refs):
    views, groups, order, n_col = (opts[k] for k in ("views", "groups", "order", "n_col"))
    by_xor, count = opts["by_xor"], len(views)
    arrays, refs = refs[: opts["lefts"]], refs[opts["lefts"] :]
    sources, refs = refs[: opts["sources"]], refs[opts["sources"] :]
    before = refs[0] if opts["before"] else None
    *outs, left, right, total, left_sems, sems = refs[opts["before"] + opts["held"] :]
    row, me = where[0], where[1]
    sub = right.shape[2] // 2
    depth = right.shape[1] // n_col
    first = groups[0][0] * sub
    step, third = pl.program_id(0), pl.program_id(1)

    def left_copies(c):
        found, at = [], 0
        for g, group in enumerate(groups):
            source = arrays[g * n_col + c] if by_xor else arrays[g].at[c]
            lanes = pl.ds(at, len(group) * sub)
            found.append(pltpu.make_async_copy(source, left.at[c, :, :, lanes], left_sems.at[g, c]))
            at += len(group) * sub
        return found

    def right_copies(t, s, lane, c):
        block = me ^ c if by_xor else c
        start = pl.multiple_of(block * depth, 32) if by_xor else block * depth
        found = []
        for p in range(2):
            source, lanes = sources[s], pl.ds(lane, sub)
            if len(source.shape) == 4:
                rows = source.at[block, p, pl.ds(first, depth), lanes]
            elif source.shape[1] == NS:
                rows = source.at[p, pl.ds(pl.multiple_of(block * sub * THIRDS + first, 32), depth), lanes]
            else:
                rows = source.at[p, pl.ds(first, depth), lanes]
            target = right.at[t, pl.ds(start, depth), pl.ds(p * sub, sub)]
            found.append(pltpu.make_async_copy(rows, target, sems.at[t, p, c]))
        return found

    def start_all(c):
        for copy in left_copies(c):
            copy.start()
        for t, (found, lane) in enumerate(views):
            for s, up in found:
                if up is None:
                    for copy in right_copies(t, s, lane, c):
                        copy.start()
                    continue

                @pl.when(row + up == (me ^ c if by_xor else c))
                def _(t=t, s=s, lane=lane):
                    for copy in right_copies(t, s, lane, c):
                        copy.start()

    for c in range(n_col):

        @pl.when((third == 0) & (step == c))
        def _(c=c):
            if c == 0:
                start_all(0)
            if c + 1 < n_col:
                start_all(c + 1)
            for copy in left_copies(c):
                copy.wait()

        for t, (found, lane) in enumerate(views):

            @pl.when((third == t) & (step == c))
            def _(c=c, t=t, s=found[0][0], lane=lane):
                for copy in right_copies(t, s, lane, c):
                    copy.wait()

    block = me ^ step if by_xor else step
    rows = right[third, pl.ds(pl.multiple_of(block * depth, 32), depth), :]

    @pl.when(step == 0)
    def _():
        for p in range(2):
            total[third, p] = jnp.dot(left[step, p], rows, preferred_element_type=F32)

    @pl.when(step > 0)
    def _():
        for p in range(2):
            total[third, p] += jnp.dot(left[step, p], rows, preferred_element_type=F32)

    @pl.when(step == n_col - 1)
    def _():
        real = total[third, 0, :, :sub] - total[third, 1, :, sub:]
        imag = total[third, 0, :, sub:] + total[third, 1, :, :sub]
        for p, value in enumerate((real, imag)):
            if before is not None:
                value = value + before[p]
            if order is None:
                outs[0][p] = value
                continue
            value = (value * opts["weight"]).astype(BF16)
            outs[0][0, p] = value
            if len(outs) > 1:
                outs[1][p] = value


def complex_product(where, lefts, sources, views, shape, held, at, before=None):
    groups = [group for _, group in lefts]
    by_xor = isinstance(lefts[0][0], list)
    arrays = [a for pieces, _ in lefts for a in pieces] if by_xor else [a for a, _ in lefts]
    n_col = len(lefts[0][0]) if by_xor else arrays[0].shape[0]
    rows = arrays[0].shape[-2]
    sub = arrays[0].shape[-1] // len(groups[0])
    lanes = sum(len(g) for g in groups) * sub
    order, count = None, len(views)

    def late(c, t):
        return jnp.where(c == n_col - 1, t, 0)

    if at is None:
        out_specs = [pl.BlockSpec((2, rows, sub), lambda c, t, s: (0, 0, late(c, t)))]
        out_shape = [jax.ShapeDtypeStruct((2, rows, count * sub), F32)]
    else:
        order, f, third = at
        out_specs = [pl.BlockSpec((1, 2, rows, sub), lambda c, t, s: (order, f, 0, third + late(c, t)))]
        out_shape = [jax.ShapeDtypeStruct(shape, BF16)]
        if order == 0:
            out_specs.append(pl.BlockSpec((2, rows, sub), lambda c, t, s: (0, 0, late(c, t))))
            out_shape.append(jax.ShapeDtypeStruct((2, rows, count * sub), BF16))
    in_specs = [pl.BlockSpec(memory_space=pl.ANY)] * (len(arrays) + len(sources))
    args = [*arrays, *sources]
    if before is not None:
        in_specs.append(pl.BlockSpec((2, rows, sub), lambda c, t, s: (0, 0, late(c, t))))
        args.append(before)
    aliases = {1 + len(args) + k: k for k in range(len(held))}
    in_specs += [pl.BlockSpec(memory_space=pl.ANY)] * len(held)
    opts = dict(
        views=views,
        groups=groups,
        order=order,
        n_col=n_col,
        lefts=len(arrays),
        sources=len(sources),
        by_xor=by_xor,
        weight=1.0 / math.sqrt(2.0 * NS),
        before=int(before is not None),
        held=len(held),
    )
    return pl.pallas_call(
        functools.partial(product_kernel, opts),
        grid_spec=pltpu.PrefetchScalarGridSpec(
            num_scalar_prefetch=1,
            grid=(n_col, count),
            in_specs=in_specs,
            out_specs=out_specs,
            scratch_shapes=[
                pltpu.VMEM((n_col, 2, rows, lanes), BF16),
                pltpu.VMEM((count, lanes * n_col, 2 * sub), BF16),
                pltpu.VMEM((count, 2, rows, 2 * sub), F32),
                pltpu.SemaphoreType.DMA((len(groups), n_col)),
                pltpu.SemaphoreType.DMA((count, 2, n_col)),
            ],
        ),
        out_shape=out_shape,
        input_output_aliases=aliases,
        compiler_params=pltpu.CompilerParams(vmem_limit_bytes=(44 if count > 1 else 24) * 2**20),
        cost_estimate=CHEAP,
    )(where, *args, *held)


def per_device(acq_data, grid_row, counts):
    n_row = lax.axis_size("row")
    n_col = lax.axis_size("col")
    own_cap, planes, order = acq_data.shape
    block_rows = order // n_row
    tile_cols = order // n_col
    cap = own_cap // n_row
    slots = n_row * cap
    wide = 2 * tile_cols // THIRDS
    everything = tuple(range(THIRDS))

    slot_index = jnp.arange(own_cap, dtype=jnp.int32)
    block = jnp.where(slot_index < counts[0], grid_row // block_rows, n_row)
    earlier = (block[None, :] == block[:, None]) & (slot_index[None, :] < slot_index[:, None])
    rank = jnp.sum(earlier.astype(jnp.int32), axis=1)
    leaving = jnp.where(block < n_row, block * cap + rank, -1)
    hit = jnp.arange(slots, dtype=jnp.int32)[:, None] == leaving[None, :]
    spots = jnp.sum(jnp.where(hit, (grid_row % block_rows)[None, :] + 1, 0), axis=1) - 1
    picker = hit.astype(BF16)
    data = jnp.transpose(acq_data, (1, 0, 2))
    line = n_row <= 4 and block_rows == tile_cols
    my_row = lax.axis_index("row")
    labels = jnp.broadcast_to(spots.reshape(n_row, 1, cap), (n_row, n_col, cap))
    places = lax.all_to_all(
        labels.reshape(n_row * n_col, cap), ("row", "col"), split_axis=0, concat_axis=0, tiled=True
    ).reshape(-1)
    placer = (jnp.arange(block_rows, dtype=jnp.int32)[:, None] == places[None, :]).astype(BF16)

    tiles, lefts = [], []
    pair = None
    sent = [bin_rows(picker, data, f, n_row, n_col) for f in range(FREQ)]
    sent[0] = after(sent[0], places)
    for f in range(FREQ):
        got = lax.all_to_all(
            sent[f].reshape(n_row * n_col, cap, 2 * tile_cols), ("row", "col"), split_axis=0, concat_axis=0, tiled=True
        ).reshape(-1, 2 * tile_cols)
        if f == 0:
            got = after(got, sent[1])
        if pair is not None:
            got, pair, _ = lax.optimization_barrier((got, pair, lefts[0][0]))
        tile, *cut = place_rows(placer, got, (THIRDS - 1, 1) if f else ())
        if line and f == 0:
            pair = hop((tile, tile), 1, n_row)
        tiles.append(tile)
        if f == 0:
            lefts.append((lax.all_gather(tile, "col", axis=0), everything))

    def gather_rows(part):
        if block_rows == tile_cols:
            return lax.all_gather(part, "row", axis=0)
        return lax.all_gather(part, "row", axis=1, tiled=True)

    sub = tile_cols // THIRDS
    views1 = [([(0, None)], j * sub) for j in everything[:-1]] + [([(1, None)], 0)]
    second = None
    if line:
        right0, ups = [tiles[0], *pair], [0, 1, -1]
        for k in range(2, n_row):
            pair = hop(pair, k, n_row)
            second = pair if k == 2 else second
            right0 += list(pair)
            ups += [k, -k]
        cut[1] = after(cut[1], second)
    else:
        right0, ups = [gather_rows(tiles[0])], [None]
    right1 = [gather_rows(part) for part in cut]
    lefts.append((gather_cols(tiles[1], n_col, pair), everything))
    views0 = [(list(enumerate(ups)), j * sub) for j in everything]

    where = jnp.stack([my_row, lax.axis_index("col")]).astype(jnp.int32)
    product = functools.partial(complex_product, where)
    shape = (2, planes, block_rows, tile_cols)
    result, piece = product([lefts[0]], right0, views0, shape, (), (0, 0, 0))
    result, most = product([lefts[1]], right1[:1], views1[:-1], shape, (result,), (0, 1, 0))
    found = gather_cols(piece, n_col, most)
    result, rest = product([lefts[1]], right1[1:], [([(0, None)], 0)], shape, (result,), (0, 1, THIRDS - 1))
    (result,) = product([(found, everything)], right0, views0, shape, (result,), (1, 0, 0))
    most = gather_cols(most, n_col, result)
    (sums,) = product([(most, everything[:-1])], right1, views1, shape, (), None)
    rest = gather_cols(rest, n_col, sums)
    return product([(rest, everything[-1:])], right1, views1, shape, (result,), (1, 1, 0), before=sums)[0]


def solution(mesh):
    placed = (
        P(("groups", "row", "col"), None, None),
        P(("groups", "row", "col")),
        P(("groups", "row", "col")),
    )
    return jax.shard_map(
        per_device,
        mesh=mesh,
        in_specs=placed,
        out_specs=P("groups", None, "row", "col"),
        check_vma=False,
    )
```

```python
import functools
import math

import jax
import jax.numpy as jnp
from jax import lax
from jax.experimental import pallas as pl
from jax.experimental.pallas import tpu as pltpu
from jax.sharding import PartitionSpec as P

NS = 3072
FREQ = 2
THIRDS = 3
BF16 = jnp.bfloat16
F32 = jnp.float32


def hop(pair, k, n_row):
    down = [(r, r - 1) for r in range(1, n_row) if r + k - 1 < n_row]
    up = [(r, r + 1) for r in range(n_row - 1) if r - k + 1 >= 0]
    return lax.ppermute(pair[0], "row", down), lax.ppermute(pair[1], "row", up)


CHEAP = pl.CostEstimate(flops=1000, bytes_accessed=1000, transcendentals=0)


def bin_kernel(picker, data, out):
    n_row, cap = out.shape[0], out.shape[2]
    cols = data.shape[2]
    for p in range(2):
        rows = jnp.dot(picker[...], data[p], preferred_element_type=F32).astype(BF16)
        for b in range(n_row):
            out[b, 0, :, p * cols : (p + 1) * cols] = rows[b * cap : (b + 1) * cap]


def bin_rows(picker, data, f, n_row, n_col):
    planes, own_cap, order = data.shape
    cap = picker.shape[0] // n_row
    cols = order // n_col
    return pl.pallas_call(
        bin_kernel,
        grid=(n_col,),
        in_specs=[
            pl.BlockSpec(picker.shape, lambda c: (0, 0)),
            pl.BlockSpec((2, own_cap, cols), lambda c: (f, 0, c)),
        ],
        out_specs=pl.BlockSpec((n_row, 1, cap, 2 * cols), lambda c: (0, c, 0, 0)),
        out_shape=jax.ShapeDtypeStruct((n_row, n_col, cap, 2 * cols), BF16),
        compiler_params=pltpu.CompilerParams(vmem_limit_bytes=24 * 2**20),
        cost_estimate=CHEAP,
    )(picker, data)


def place_kernel(placer, got, tile, *parts):
    rows = jnp.dot(placer[...], got[...], preferred_element_type=F32).astype(BF16)
    tile[0] = rows
    at = 0
    for part in parts:
        part[0] = rows[:, at : at + part.shape[2]]
        at += part.shape[2]


def place_rows(placer, got, parts):
    block_rows, arrived = placer.shape
    cols = got.shape[1] // 2
    sizes = [cols] + [n * cols // THIRDS for n in parts]
    return pl.pallas_call(
        place_kernel,
        grid=(2,),
        in_specs=[
            pl.BlockSpec(placer.shape, lambda p: (0, 0)),
            pl.BlockSpec((arrived, cols), lambda p: (0, p)),
        ],
        out_specs=[pl.BlockSpec((1, block_rows, n), lambda p: (p, 0, 0)) for n in sizes],
        out_shape=[jax.ShapeDtypeStruct((2, block_rows, n), BF16) for n in sizes],
        compiler_params=pltpu.CompilerParams(vmem_limit_bytes=32 * 2**20),
        cost_estimate=CHEAP,
    )(placer, got)


def after(value, earlier):
    return lax.optimization_barrier((value, earlier))[0]


def gather_cols(piece, n_col, second_after=None):
    held = {0: piece}
    bit = n_col // 2
    while bit:
        if second_after is not None and len(held) == 2:
            held = {d: after(a, second_after) for d, a in held.items()}
        pairs = [(c, c ^ bit) for c in range(n_col)]
        arrived = {d ^ bit: lax.ppermute(a, "col", pairs) for d, a in held.items()}
        held.update(arrived)
        bit //= 2
    return [held[d] for d in range(n_col)]


def product_kernel(opts, where, *refs):
    views, groups, order, n_col = (opts[k] for k in ("views", "groups", "order", "n_col"))
    by_xor, count = opts["by_xor"], len(views)
    arrays, refs = refs[: opts["lefts"]], refs[opts["lefts"] :]
    sources, refs = refs[: opts["sources"]], refs[opts["sources"] :]
    before = refs[0] if opts["before"] else None
    *outs, left, right, total, left_sems, sems = refs[opts["before"] + opts["held"] :]
    row, me = where[0], where[1]
    sub = right.shape[2] // 2
    depth = right.shape[1] // n_col
    first = groups[0][0] * sub
    step, third = pl.program_id(0), pl.program_id(1)

    def left_copies(c):
        found, at = [], 0
        for g, group in enumerate(groups):
            source = arrays[g * n_col + c] if by_xor else arrays[g].at[c]
            lanes = pl.ds(at, len(group) * sub)
            found.append(pltpu.make_async_copy(source, left.at[c, :, :, lanes], left_sems.at[g, c]))
            at += len(group) * sub
        return found

    def right_copies(t, s, lane, c):
        block = me ^ c if by_xor else c
        start = pl.multiple_of(block * depth, 32) if by_xor else block * depth
        found = []
        for p in range(2):
            source, lanes = sources[s], pl.ds(lane, sub)
            if len(source.shape) == 4:
                rows = source.at[block, p, pl.ds(first, depth), lanes]
            elif source.shape[1] == NS:
                rows = source.at[p, pl.ds(pl.multiple_of(block * sub * THIRDS + first, 32), depth), lanes]
            else:
                rows = source.at[p, pl.ds(first, depth), lanes]
            target = right.at[t, pl.ds(start, depth), pl.ds(p * sub, sub)]
            found.append(pltpu.make_async_copy(rows, target, sems.at[t, p, c]))
        return found

    def start_all(c):
        for copy in left_copies(c):
            copy.start()
        for t, (found, lane) in enumerate(views):
            for s, up in found:
                if up is None:
                    for copy in right_copies(t, s, lane, c):
                        copy.start()
                    continue

                @pl.when(row + up == (me ^ c if by_xor else c))
                def _(t=t, s=s, lane=lane):
                    for copy in right_copies(t, s, lane, c):
                        copy.start()

    for c in range(n_col):

        @pl.when((third == 0) & (step == c))
        def _(c=c):
            if c == 0:
                start_all(0)
            if c + 1 < n_col:
                start_all(c + 1)
            for copy in left_copies(c):
                copy.wait()

        for t, (found, lane) in enumerate(views):

            @pl.when((third == t) & (step == c))
            def _(c=c, t=t, s=found[0][0], lane=lane):
                for copy in right_copies(t, s, lane, c):
                    copy.wait()

    block = me ^ step if by_xor else step
    rows = right[third, pl.ds(pl.multiple_of(block * depth, 32), depth), :]

    @pl.when(step == 0)
    def _():
        for p in range(2):
            total[third, p] = jnp.dot(left[step, p], rows, preferred_element_type=F32)

    @pl.when(step > 0)
    def _():
        for p in range(2):
            total[third, p] += jnp.dot(left[step, p], rows, preferred_element_type=F32)

    @pl.when(step == n_col - 1)
    def _():
        real = total[third, 0, :, :sub] - total[third, 1, :, sub:]
        imag = total[third, 0, :, sub:] + total[third, 1, :, :sub]
        for p, value in enumerate((real, imag)):
            if before is not None:
                value = value + before[p]
            if order is None:
                outs[0][p] = value
                continue
            value = (value * opts["weight"]).astype(BF16)
            outs[0][0, p] = value
            if len(outs) > 1:
                outs[1][p] = value


def complex_product(where, lefts, sources, views, shape, held, at, before=None):
    groups = [group for _, group in lefts]
    by_xor = isinstance(lefts[0][0], list)
    arrays = [a for pieces, _ in lefts for a in pieces] if by_xor else [a for a, _ in lefts]
    n_col = len(lefts[0][0]) if by_xor else arrays[0].shape[0]
    rows = arrays[0].shape[-2]
    sub = arrays[0].shape[-1] // len(groups[0])
    lanes = sum(len(g) for g in groups) * sub
    order, count = None, len(views)

    def late(c, t):
        return jnp.where(c == n_col - 1, t, 0)

    if at is None:
        out_specs = [pl.BlockSpec((2, rows, sub), lambda c, t, s: (0, 0, late(c, t)))]
        out_shape = [jax.ShapeDtypeStruct((2, rows, count * sub), F32)]
    else:
        order, f, third = at
        out_specs = [pl.BlockSpec((1, 2, rows, sub), lambda c, t, s: (order, f, 0, third + late(c, t)))]
        out_shape = [jax.ShapeDtypeStruct(shape, BF16)]
        if order == 0:
            out_specs.append(pl.BlockSpec((2, rows, sub), lambda c, t, s: (0, 0, late(c, t))))
            out_shape.append(jax.ShapeDtypeStruct((2, rows, count * sub), BF16))
    in_specs = [pl.BlockSpec(memory_space=pl.ANY)] * (len(arrays) + len(sources))
    args = [*arrays, *sources]
    if before is not None:
        in_specs.append(pl.BlockSpec((2, rows, sub), lambda c, t, s: (0, 0, late(c, t))))
        args.append(before)
    aliases = {1 + len(args) + k: k for k in range(len(held))}
    in_specs += [pl.BlockSpec(memory_space=pl.ANY)] * len(held)
    opts = dict(
        views=views,
        groups=groups,
        order=order,
        n_col=n_col,
        lefts=len(arrays),
        sources=len(sources),
        by_xor=by_xor,
        weight=1.0 / math.sqrt(2.0 * NS),
        before=int(before is not None),
        held=len(held),
    )
    return pl.pallas_call(
        functools.partial(product_kernel, opts),
        grid_spec=pltpu.PrefetchScalarGridSpec(
            num_scalar_prefetch=1,
            grid=(n_col, count),
            in_specs=in_specs,
            out_specs=out_specs,
            scratch_shapes=[
                pltpu.VMEM((n_col, 2, rows, lanes), BF16),
                pltpu.VMEM((count, lanes * n_col, 2 * sub), BF16),
                pltpu.VMEM((count, 2, rows, 2 * sub), F32),
                pltpu.SemaphoreType.DMA((len(groups), n_col)),
                pltpu.SemaphoreType.DMA((count, 2, n_col)),
            ],
        ),
        out_shape=out_shape,
        input_output_aliases=aliases,
        compiler_params=pltpu.CompilerParams(vmem_limit_bytes=(44 if count > 1 else 24) * 2**20),
        cost_estimate=CHEAP,
    )(where, *args, *held)


def per_device(acq_data, grid_row, counts):
    n_row = lax.axis_size("row")
    n_col = lax.axis_size("col")
    own_cap, planes, order = acq_data.shape
    block_rows = order // n_row
    tile_cols = order // n_col
    cap = own_cap // n_row
    slots = n_row * cap
    wide = 2 * tile_cols // THIRDS
    everything = tuple(range(THIRDS))

    slot_index = jnp.arange(own_cap, dtype=jnp.int32)
    block = jnp.where(slot_index < counts[0], grid_row // block_rows, n_row)
    earlier = (block[None, :] == block[:, None]) & (slot_index[None, :] < slot_index[:, None])
    rank = jnp.sum(earlier.astype(jnp.int32), axis=1)
    leaving = jnp.where(block < n_row, block * cap + rank, -1)
    hit = jnp.arange(slots, dtype=jnp.int32)[:, None] == leaving[None, :]
    spots = jnp.sum(jnp.where(hit, (grid_row % block_rows)[None, :] + 1, 0), axis=1) - 1
    picker = hit.astype(BF16)
    data = jnp.transpose(acq_data, (1, 0, 2))
    line = n_row <= 4 and block_rows == tile_cols
    my_row = lax.axis_index("row")
    labels = jnp.broadcast_to(spots.reshape(n_row, 1, cap), (n_row, n_col, cap))
    places = lax.all_to_all(
        labels.reshape(n_row * n_col, cap), ("row", "col"), split_axis=0, concat_axis=0, tiled=True
    ).reshape(-1)
    placer = (jnp.arange(block_rows, dtype=jnp.int32)[:, None] == places[None, :]).astype(BF16)

    tiles, lefts = [], []
    pair = None
    sent = [bin_rows(picker, data, f, n_row, n_col) for f in range(FREQ)]
    sent[0] = after(sent[0], places)
    for f in range(FREQ):
        got = lax.all_to_all(
            sent[f].reshape(n_row * n_col, cap, 2 * tile_cols), ("row", "col"), split_axis=0, concat_axis=0, tiled=True
        ).reshape(-1, 2 * tile_cols)
        if f == 0:
            got = after(got, sent[1])
        if pair is not None:
            got, pair, _ = lax.optimization_barrier((got, pair, lefts[0][0]))
        tile, *cut = place_rows(placer, got, (THIRDS - 1, 1) if f else ())
        if line and f == 0:
            pair = hop((tile, tile), 1, n_row)
        tiles.append(tile)
        if f == 0:
            lefts.append((lax.all_gather(tile, "col", axis=0), everything))

    def gather_rows(part):
        if block_rows == tile_cols:
            return lax.all_gather(part, "row", axis=0)
        return lax.all_gather(part, "row", axis=1, tiled=True)

    sub = tile_cols // THIRDS
    views1 = [([(0, None)], j * sub) for j in everything[:-1]] + [([(1, None)], 0)]
    if line:
        right0, ups = [tiles[0], *pair], [0, 1, -1]
        for k in range(2, n_row):
            pair = hop(pair, k, n_row)
            right0 += list(pair)
            ups += [k, -k]
        cut = [after(part, pair) for part in cut]
    else:
        right0, ups = [gather_rows(tiles[0])], [None]
    right1 = [gather_rows(part) for part in cut]
    lefts.append((gather_cols(tiles[1], n_col, pair), everything))
    views0 = [(list(enumerate(ups)), j * sub) for j in everything]

    where = jnp.stack([my_row, lax.axis_index("col")]).astype(jnp.int32)
    product = functools.partial(complex_product, where)
    shape = (2, planes, block_rows, tile_cols)
    result, piece = product([lefts[0]], right0, views0, shape, (), (0, 0, 0))
    found = gather_cols(piece, n_col)
    (result,) = product([(found, everything)], right0, views0, shape, (result,), (1, 0, 0))
    result, most = product([lefts[1]], right1[:1], views1[:-1], shape, (result,), (0, 1, 0))
    most = gather_cols(most, n_col)
    result, rest = product([lefts[1]], right1[1:], [([(0, None)], 0)], shape, (result,), (0, 1, THIRDS - 1))
    (sums,) = product([(most, everything[:-1])], right1, views1, shape, (), None)
    rest = gather_cols(rest, n_col, sums)
    return product([(rest, everything[-1:])], right1, views1, shape, (result,), (1, 1, 0), before=sums)[0]


def solution(mesh):
    placed = (
        P(("groups", "row", "col"), None, None),
        P(("groups", "row", "col")),
        P(("groups", "row", "col")),
    )
    return jax.shard_map(
        per_device,
        mesh=mesh,
        in_specs=placed,
        out_specs=P("groups", None, "row", "col"),
        check_vma=False,
    )
```

```python
import functools
import math

import jax
import jax.numpy as jnp
from jax import lax
from jax.experimental import pallas as pl
from jax.experimental.pallas import tpu as pltpu
from jax.sharding import PartitionSpec as P

NS = 3072
FREQ = 2
THIRDS = 3
BF16 = jnp.bfloat16
F32 = jnp.float32


def hop(pair, k, n_row):
    down = [(r, r - 1) for r in range(1, n_row) if r + k - 1 < n_row]
    up = [(r, r + 1) for r in range(n_row - 1) if r - k + 1 >= 0]
    return lax.ppermute(pair[0], "row", down), lax.ppermute(pair[1], "row", up)


CHEAP = pl.CostEstimate(flops=1000, bytes_accessed=1000, transcendentals=0)


def bin_kernel(picker, data, out):
    n_row, cap = out.shape[0], out.shape[2]
    cols = data.shape[2]
    for p in range(2):
        rows = jnp.dot(picker[...], data[p], preferred_element_type=F32).astype(BF16)
        for b in range(n_row):
            out[b, 0, :, p * cols : (p + 1) * cols] = rows[b * cap : (b + 1) * cap]


def bin_rows(picker, data, f, n_row, n_col):
    planes, own_cap, order = data.shape
    cap = picker.shape[0] // n_row
    cols = order // n_col
    return pl.pallas_call(
        bin_kernel,
        grid=(n_col,),
        in_specs=[
            pl.BlockSpec(picker.shape, lambda c: (0, 0)),
            pl.BlockSpec((2, own_cap, cols), lambda c: (f, 0, c)),
        ],
        out_specs=pl.BlockSpec((n_row, 1, cap, 2 * cols), lambda c: (0, c, 0, 0)),
        out_shape=jax.ShapeDtypeStruct((n_row, n_col, cap, 2 * cols), BF16),
        compiler_params=pltpu.CompilerParams(vmem_limit_bytes=24 * 2**20),
        cost_estimate=CHEAP,
    )(picker, data)


def place_kernel(placer, got, tile, *parts):
    rows = jnp.dot(placer[...], got[...], preferred_element_type=F32).astype(BF16)
    tile[0] = rows
    at = 0
    for part in parts:
        part[0] = rows[:, at : at + part.shape[2]]
        at += part.shape[2]


def place_rows(placer, got, parts):
    block_rows, arrived = placer.shape
    cols = got.shape[1] // 2
    sizes = [cols] + [n * cols // THIRDS for n in parts]
    return pl.pallas_call(
        place_kernel,
        grid=(2,),
        in_specs=[
            pl.BlockSpec(placer.shape, lambda p: (0, 0)),
            pl.BlockSpec((arrived, cols), lambda p: (0, p)),
        ],
        out_specs=[pl.BlockSpec((1, block_rows, n), lambda p: (p, 0, 0)) for n in sizes],
        out_shape=[jax.ShapeDtypeStruct((2, block_rows, n), BF16) for n in sizes],
        compiler_params=pltpu.CompilerParams(vmem_limit_bytes=32 * 2**20),
        cost_estimate=CHEAP,
    )(placer, got)


def after(value, earlier):
    return lax.optimization_barrier((value, earlier))[0]


def gather_cols(piece, n_col, second_after=None):
    held = {0: piece}
    bit = n_col // 2
    while bit:
        if second_after is not None and len(held) == 2:
            held = {d: after(a, second_after) for d, a in held.items()}
        pairs = [(c, c ^ bit) for c in range(n_col)]
        arrived = {d ^ bit: lax.ppermute(a, "col", pairs) for d, a in held.items()}
        held.update(arrived)
        bit //= 2
    return [held[d] for d in range(n_col)]


def product_kernel(opts, where, *refs):
    views, groups, order, n_col = (opts[k] for k in ("views", "groups", "order", "n_col"))
    by_xor, count = opts["by_xor"], len(views)
    arrays, refs = refs[: opts["lefts"]], refs[opts["lefts"] :]
    sources, refs = refs[: opts["sources"]], refs[opts["sources"] :]
    before = refs[0] if opts["before"] else None
    *outs, left, right, total, left_sems, sems = refs[opts["before"] + opts["held"] :]
    row, me = where[0], where[1]
    sub = right.shape[2] // 2
    depth = right.shape[1] // n_col
    first = groups[0][0] * sub
    step, third = pl.program_id(0), pl.program_id(1)

    def left_copies(c):
        found, at = [], 0
        for g, group in enumerate(groups):
            source = arrays[g * n_col + c] if by_xor else arrays[g].at[c]
            lanes = pl.ds(at, len(group) * sub)
            found.append(pltpu.make_async_copy(source, left.at[c, :, :, lanes], left_sems.at[g, c]))
            at += len(group) * sub
        return found

    def right_copies(t, s, lane, c):
        block = me ^ c if by_xor else c
        start = pl.multiple_of(block * depth, 32) if by_xor else block * depth
        found = []
        for p in range(2):
            source, lanes = sources[s], pl.ds(lane, sub)
            if len(source.shape) == 4:
                rows = source.at[block, p, pl.ds(first, depth), lanes]
            elif source.shape[1] == NS:
                rows = source.at[p, pl.ds(pl.multiple_of(block * sub * THIRDS + first, 32), depth), lanes]
            else:
                rows = source.at[p, pl.ds(first, depth), lanes]
            target = right.at[t, pl.ds(start, depth), pl.ds(p * sub, sub)]
            found.append(pltpu.make_async_copy(rows, target, sems.at[t, p, c]))
        return found

    def start_all(c):
        for copy in left_copies(c):
            copy.start()
        for t, (found, lane) in enumerate(views):
            for s, up in found:
                if up is None:
                    for copy in right_copies(t, s, lane, c):
                        copy.start()
                    continue

                @pl.when(row + up == (me ^ c if by_xor else c))
                def _(t=t, s=s, lane=lane):
                    for copy in right_copies(t, s, lane, c):
                        copy.start()

    for c in range(n_col):

        @pl.when((third == 0) & (step == c))
        def _(c=c):
            if c == 0:
                start_all(0)
            if c + 1 < n_col:
                start_all(c + 1)
            for copy in left_copies(c):
                copy.wait()

        for t, (found, lane) in enumerate(views):

            @pl.when((third == t) & (step == c))
            def _(c=c, t=t, s=found[0][0], lane=lane):
                for copy in right_copies(t, s, lane, c):
                    copy.wait()

    block = me ^ step if by_xor else step
    rows = right[third, pl.ds(pl.multiple_of(block * depth, 32), depth), :]

    @pl.when(step == 0)
    def _():
        for p in range(2):
            total[third, p] = jnp.dot(left[step, p], rows, preferred_element_type=F32)

    @pl.when(step > 0)
    def _():
        for p in range(2):
            total[third, p] += jnp.dot(left[step, p], rows, preferred_element_type=F32)

    @pl.when(step == n_col - 1)
    def _():
        real = total[third, 0, :, :sub] - total[third, 1, :, sub:]
        imag = total[third, 0, :, sub:] + total[third, 1, :, :sub]
        for p, value in enumerate((real, imag)):
            if before is not None:
                value = value + before[p]
            if order is None:
                outs[0][p] = value
                continue
            value = (value * opts["weight"]).astype(BF16)
            outs[0][0, p] = value
            if len(outs) > 1:
                outs[1][p] = value


def complex_product(where, lefts, sources, views, shape, held, at, before=None):
    groups = [group for _, group in lefts]
    by_xor = isinstance(lefts[0][0], list)
    arrays = [a for pieces, _ in lefts for a in pieces] if by_xor else [a for a, _ in lefts]
    n_col = len(lefts[0][0]) if by_xor else arrays[0].shape[0]
    rows = arrays[0].shape[-2]
    sub = arrays[0].shape[-1] // len(groups[0])
    lanes = sum(len(g) for g in groups) * sub
    order, count = None, len(views)

    def late(c, t):
        return jnp.where(c == n_col - 1, t, 0)

    if at is None:
        out_specs = [pl.BlockSpec((2, rows, sub), lambda c, t, s: (0, 0, late(c, t)))]
        out_shape = [jax.ShapeDtypeStruct((2, rows, count * sub), F32)]
    else:
        order, f, third = at
        out_specs = [pl.BlockSpec((1, 2, rows, sub), lambda c, t, s: (order, f, 0, third + late(c, t)))]
        out_shape = [jax.ShapeDtypeStruct(shape, BF16)]
        if order == 0:
            out_specs.append(pl.BlockSpec((2, rows, sub), lambda c, t, s: (0, 0, late(c, t))))
            out_shape.append(jax.ShapeDtypeStruct((2, rows, count * sub), BF16))
    in_specs = [pl.BlockSpec(memory_space=pl.ANY)] * (len(arrays) + len(sources))
    args = [*arrays, *sources]
    if before is not None:
        in_specs.append(pl.BlockSpec((2, rows, sub), lambda c, t, s: (0, 0, late(c, t))))
        args.append(before)
    aliases = {1 + len(args) + k: k for k in range(len(held))}
    in_specs += [pl.BlockSpec(memory_space=pl.ANY)] * len(held)
    opts = dict(
        views=views,
        groups=groups,
        order=order,
        n_col=n_col,
        lefts=len(arrays),
        sources=len(sources),
        by_xor=by_xor,
        weight=1.0 / math.sqrt(2.0 * NS),
        before=int(before is not None),
        held=len(held),
    )
    return pl.pallas_call(
        functools.partial(product_kernel, opts),
        grid_spec=pltpu.PrefetchScalarGridSpec(
            num_scalar_prefetch=1,
            grid=(n_col, count),
            in_specs=in_specs,
            out_specs=out_specs,
            scratch_shapes=[
                pltpu.VMEM((n_col, 2, rows, lanes), BF16),
                pltpu.VMEM((count, lanes * n_col, 2 * sub), BF16),
                pltpu.VMEM((count, 2, rows, 2 * sub), F32),
                pltpu.SemaphoreType.DMA((len(groups), n_col)),
                pltpu.SemaphoreType.DMA((count, 2, n_col)),
            ],
        ),
        out_shape=out_shape,
        input_output_aliases=aliases,
        compiler_params=pltpu.CompilerParams(vmem_limit_bytes=(44 if count > 1 else 24) * 2**20),
        cost_estimate=CHEAP,
    )(where, *args, *held)


def per_device(acq_data, grid_row, counts):
    n_row = lax.axis_size("row")
    n_col = lax.axis_size("col")
    own_cap, planes, order = acq_data.shape
    block_rows = order // n_row
    tile_cols = order // n_col
    cap = own_cap // n_row
    slots = n_row * cap
    wide = 2 * tile_cols // THIRDS
    everything = tuple(range(THIRDS))

    slot_index = jnp.arange(own_cap, dtype=jnp.int32)
    block = jnp.where(slot_index < counts[0], grid_row // block_rows, n_row)
    earlier = (block[None, :] == block[:, None]) & (slot_index[None, :] < slot_index[:, None])
    rank = jnp.sum(earlier.astype(jnp.int32), axis=1)
    leaving = jnp.where(block < n_row, block * cap + rank, -1)
    hit = jnp.arange(slots, dtype=jnp.int32)[:, None] == leaving[None, :]
    spots = jnp.sum(jnp.where(hit, (grid_row % block_rows)[None, :] + 1, 0), axis=1) - 1
    picker = hit.astype(BF16)
    data = jnp.transpose(acq_data, (1, 0, 2))
    line = n_row <= 4 and block_rows == tile_cols
    my_row = lax.axis_index("row")
    labels = jnp.broadcast_to(spots.reshape(n_row, 1, cap), (n_row, n_col, cap))
    places = lax.all_to_all(
        labels.reshape(n_row * n_col, cap), ("row", "col"), split_axis=0, concat_axis=0, tiled=True
    ).reshape(-1)
    placer = (jnp.arange(block_rows, dtype=jnp.int32)[:, None] == places[None, :]).astype(BF16)

    tiles, lefts = [], []
    pair = None
    sent = [bin_rows(picker, data, f, n_row, n_col) for f in range(FREQ)]
    sent[0] = after(sent[0], places)
    for f in range(FREQ):
        got = lax.all_to_all(
            sent[f].reshape(n_row * n_col, cap, 2 * tile_cols), ("row", "col"), split_axis=0, concat_axis=0, tiled=True
        ).reshape(-1, 2 * tile_cols)
        if f == 0:
            got = after(got, sent[1])
        if pair is not None:
            got, pair, _ = lax.optimization_barrier((got, pair, lefts[0][0]))
        tile, *cut = place_rows(placer, got, (THIRDS - 1, 1) if f else ())
        if line and f == 0:
            pair = hop((tile, tile), 1, n_row)
        tiles.append(tile)
        if f == 0:
            lefts.append((lax.all_gather(tile, "col", axis=0), everything))

    def gather_rows(part):
        if block_rows == tile_cols:
            return lax.all_gather(part, "row", axis=0)
        return lax.all_gather(part, "row", axis=1, tiled=True)

    sub = tile_cols // THIRDS
    views1 = [([(0, None)], j * sub) for j in everything[:-1]] + [([(1, None)], 0)]
    if line:
        right0, ups = [tiles[0], *pair], [0, 1, -1]
        for k in range(2, n_row):
            pair = hop(pair, k, n_row)
            right0 += list(pair)
            ups += [k, -k]
        cut = [after(part, pair) for part in cut]
    else:
        right0, ups = [gather_rows(tiles[0])], [None]
    right1 = [gather_rows(part) for part in cut]
    lefts.append((gather_cols(tiles[1], n_col, pair), everything))
    views0 = [(list(enumerate(ups)), j * sub) for j in everything]

    where = jnp.stack([my_row, lax.axis_index("col")]).astype(jnp.int32)
    product = functools.partial(complex_product, where)
    shape = (2, planes, block_rows, tile_cols)
    result, piece = product([lefts[0]], right0, views0, shape, (), (0, 0, 0))
    found = gather_cols(piece, n_col)
    result, most = product([lefts[1]], right1[:1], views1[:-1], shape, (result,), (0, 1, 0))
    (result,) = product([(found, everything)], right0, views0, shape, (result,), (1, 0, 0))
    most = gather_cols(most, n_col, result)
    result, rest = product([lefts[1]], right1[1:], [([(0, None)], 0)], shape, (result,), (0, 1, THIRDS - 1))
    most[0] = after(most[0], rest)
    (sums,) = product([(most, everything[:-1])], right1, views1, shape, (), None)
    rest = gather_cols(rest, n_col, sums)
    return product([(rest, everything[-1:])], right1, views1, shape, (result,), (1, 1, 0), before=sums)[0]


def solution(mesh):
    placed = (
        P(("groups", "row", "col"), None, None),
        P(("groups", "row", "col")),
        P(("groups", "row", "col")),
    )
    return jax.shard_map(
        per_device,
        mesh=mesh,
        in_specs=placed,
        out_specs=P("groups", None, "row", "col"),
        check_vma=False,
    )
```

```python
import functools
import math

import jax
import jax.numpy as jnp
from jax import lax
from jax.experimental import pallas as pl
from jax.experimental.pallas import tpu as pltpu
from jax.sharding import PartitionSpec as P

NS = 3072
FREQ = 2
THIRDS = 3
BF16 = jnp.bfloat16
F32 = jnp.float32


def hop(pair, k, n_row):
    down = [(r, r - 1) for r in range(1, n_row) if r + k - 1 < n_row]
    up = [(r, r + 1) for r in range(n_row - 1) if r - k + 1 >= 0]
    return lax.ppermute(pair[0], "row", down), lax.ppermute(pair[1], "row", up)


CHEAP = pl.CostEstimate(flops=1000, bytes_accessed=1000, transcendentals=0)


def bin_kernel(picker, data, out):
    n_row, cap = out.shape[0], out.shape[2]
    cols = data.shape[2]
    for p in range(2):
        rows = jnp.dot(picker[...], data[p], preferred_element_type=F32).astype(BF16)
        for b in range(n_row):
            out[b, 0, :, p * cols : (p + 1) * cols] = rows[b * cap : (b + 1) * cap]


def bin_rows(picker, data, f, n_row, n_col):
    planes, own_cap, order = data.shape
    cap = picker.shape[0] // n_row
    cols = order // n_col
    return pl.pallas_call(
        bin_kernel,
        grid=(n_col,),
        in_specs=[
            pl.BlockSpec(picker.shape, lambda c: (0, 0)),
            pl.BlockSpec((2, own_cap, cols), lambda c: (f, 0, c)),
        ],
        out_specs=pl.BlockSpec((n_row, 1, cap, 2 * cols), lambda c: (0, c, 0, 0)),
        out_shape=jax.ShapeDtypeStruct((n_row, n_col, cap, 2 * cols), BF16),
        compiler_params=pltpu.CompilerParams(vmem_limit_bytes=24 * 2**20),
        cost_estimate=CHEAP,
    )(picker, data)


def place_kernel(placer, got, tile, *parts):
    rows = jnp.dot(placer[...], got[...], preferred_element_type=F32).astype(BF16)
    tile[0] = rows
    at = 0
    for part in parts:
        part[0] = rows[:, at : at + part.shape[2]]
        at += part.shape[2]


def place_rows(placer, got, parts):
    block_rows, arrived = placer.shape
    cols = got.shape[1] // 2
    sizes = [cols] + [n * cols // THIRDS for n in parts]
    return pl.pallas_call(
        place_kernel,
        grid=(2,),
        in_specs=[
            pl.BlockSpec(placer.shape, lambda p: (0, 0)),
            pl.BlockSpec((arrived, cols), lambda p: (0, p)),
        ],
        out_specs=[pl.BlockSpec((1, block_rows, n), lambda p: (p, 0, 0)) for n in sizes],
        out_shape=[jax.ShapeDtypeStruct((2, block_rows, n), BF16) for n in sizes],
        compiler_params=pltpu.CompilerParams(vmem_limit_bytes=32 * 2**20),
        cost_estimate=CHEAP,
    )(placer, got)


def after(value, earlier):
    return lax.optimization_barrier((value, earlier))[0]


def gather_cols(piece, n_col, second_after=None):
    held = {0: piece}
    bit = n_col // 2
    while bit:
        if second_after is not None and len(held) == 2:
            held = {d: after(a, second_after) for d, a in held.items()}
        pairs = [(c, c ^ bit) for c in range(n_col)]
        arrived = {d ^ bit: lax.ppermute(a, "col", pairs) for d, a in held.items()}
        held.update(arrived)
        bit //= 2
    return [held[d] for d in range(n_col)]


def product_kernel(opts, where, *refs):
    views, groups, order, n_col = (opts[k] for k in ("views", "groups", "order", "n_col"))
    by_xor, count = opts["by_xor"], len(views)
    arrays, refs = refs[: opts["lefts"]], refs[opts["lefts"] :]
    sources, refs = refs[: opts["sources"]], refs[opts["sources"] :]
    before = refs[0] if opts["before"] else None
    *outs, left, right, total, left_sems, sems = refs[opts["before"] + opts["held"] :]
    row, me = where[0], where[1]
    sub = right.shape[2] // 2
    depth = right.shape[1] // n_col
    first = groups[0][0] * sub
    step, third = pl.program_id(0), pl.program_id(1)

    def left_copies(c):
        found, at = [], 0
        for g, group in enumerate(groups):
            source = arrays[g * n_col + c] if by_xor else arrays[g].at[c]
            lanes = pl.ds(at, len(group) * sub)
            found.append(pltpu.make_async_copy(source, left.at[c, :, :, lanes], left_sems.at[g, c]))
            at += len(group) * sub
        return found

    def right_copies(t, s, lane, c):
        block = me ^ c if by_xor else c
        start = pl.multiple_of(block * depth, 32) if by_xor else block * depth
        found = []
        for p in range(2):
            source, lanes = sources[s], pl.ds(lane, sub)
            if len(source.shape) == 4:
                rows = source.at[block, p, pl.ds(first, depth), lanes]
            elif source.shape[1] == NS:
                rows = source.at[p, pl.ds(pl.multiple_of(block * sub * THIRDS + first, 32), depth), lanes]
            else:
                rows = source.at[p, pl.ds(first, depth), lanes]
            target = right.at[t, pl.ds(start, depth), pl.ds(p * sub, sub)]
            found.append(pltpu.make_async_copy(rows, target, sems.at[t, p, c]))
        return found

    def start_all(c):
        for copy in left_copies(c):
            copy.start()
        for t, (found, lane) in enumerate(views):
            for s, up in found:
                if up is None:
                    for copy in right_copies(t, s, lane, c):
                        copy.start()
                    continue

                @pl.when(row + up == (me ^ c if by_xor else c))
                def _(t=t, s=s, lane=lane):
                    for copy in right_copies(t, s, lane, c):
                        copy.start()

    for c in range(n_col):

        @pl.when((third == 0) & (step == c))
        def _(c=c):
            if c == 0:
                start_all(0)
            if c + 1 < n_col:
                start_all(c + 1)
            for copy in left_copies(c):
                copy.wait()

        for t, (found, lane) in enumerate(views):

            @pl.when((third == t) & (step == c))
            def _(c=c, t=t, s=found[0][0], lane=lane):
                for copy in right_copies(t, s, lane, c):
                    copy.wait()

    block = me ^ step if by_xor else step
    rows = right[third, pl.ds(pl.multiple_of(block * depth, 32), depth), :]

    @pl.when(step == 0)
    def _():
        for p in range(2):
            total[third, p] = jnp.dot(left[step, p], rows, preferred_element_type=F32)

    @pl.when(step > 0)
    def _():
        for p in range(2):
            total[third, p] += jnp.dot(left[step, p], rows, preferred_element_type=F32)

    @pl.when(step == n_col - 1)
    def _():
        real = total[third, 0, :, :sub] - total[third, 1, :, sub:]
        imag = total[third, 0, :, sub:] + total[third, 1, :, :sub]
        for p, value in enumerate((real, imag)):
            if before is not None:
                value = value + before[p]
            if order is None:
                outs[0][p] = value
                continue
            value = (value * opts["weight"]).astype(BF16)
            outs[0][0, p] = value
            if len(outs) > 1:
                outs[1][p] = value


def complex_product(where, lefts, sources, views, shape, held, at, before=None):
    groups = [group for _, group in lefts]
    by_xor = isinstance(lefts[0][0], list)
    arrays = [a for pieces, _ in lefts for a in pieces] if by_xor else [a for a, _ in lefts]
    n_col = len(lefts[0][0]) if by_xor else arrays[0].shape[0]
    rows = arrays[0].shape[-2]
    sub = arrays[0].shape[-1] // len(groups[0])
    lanes = sum(len(g) for g in groups) * sub
    order, count = None, len(views)

    def late(c, t):
        return jnp.where(c == n_col - 1, t, 0)

    if at is None:
        out_specs = [pl.BlockSpec((2, rows, sub), lambda c, t, s: (0, 0, late(c, t)))]
        out_shape = [jax.ShapeDtypeStruct((2, rows, count * sub), F32)]
    else:
        order, f, third = at
        out_specs = [pl.BlockSpec((1, 2, rows, sub), lambda c, t, s: (order, f, 0, third + late(c, t)))]
        out_shape = [jax.ShapeDtypeStruct(shape, BF16)]
        if order == 0:
            out_specs.append(pl.BlockSpec((2, rows, sub), lambda c, t, s: (0, 0, late(c, t))))
            out_shape.append(jax.ShapeDtypeStruct((2, rows, count * sub), BF16))
    in_specs = [pl.BlockSpec(memory_space=pl.ANY)] * (len(arrays) + len(sources))
    args = [*arrays, *sources]
    if before is not None:
        in_specs.append(pl.BlockSpec((2, rows, sub), lambda c, t, s: (0, 0, late(c, t))))
        args.append(before)
    aliases = {1 + len(args) + k: k for k in range(len(held))}
    in_specs += [pl.BlockSpec(memory_space=pl.ANY)] * len(held)
    opts = dict(
        views=views,
        groups=groups,
        order=order,
        n_col=n_col,
        lefts=len(arrays),
        sources=len(sources),
        by_xor=by_xor,
        weight=1.0 / math.sqrt(2.0 * NS),
        before=int(before is not None),
        held=len(held),
    )
    return pl.pallas_call(
        functools.partial(product_kernel, opts),
        grid_spec=pltpu.PrefetchScalarGridSpec(
            num_scalar_prefetch=1,
            grid=(n_col, count),
            in_specs=in_specs,
            out_specs=out_specs,
            scratch_shapes=[
                pltpu.VMEM((n_col, 2, rows, lanes), BF16),
                pltpu.VMEM((count, lanes * n_col, 2 * sub), BF16),
                pltpu.VMEM((count, 2, rows, 2 * sub), F32),
                pltpu.SemaphoreType.DMA((len(groups), n_col)),
                pltpu.SemaphoreType.DMA((count, 2, n_col)),
            ],
        ),
        out_shape=out_shape,
        input_output_aliases=aliases,
        compiler_params=pltpu.CompilerParams(vmem_limit_bytes=(44 if count > 1 else 24) * 2**20),
        cost_estimate=CHEAP,
    )(where, *args, *held)


def per_device(acq_data, grid_row, counts):
    n_row = lax.axis_size("row")
    n_col = lax.axis_size("col")
    own_cap, planes, order = acq_data.shape
    block_rows = order // n_row
    tile_cols = order // n_col
    cap = own_cap // n_row
    slots = n_row * cap
    wide = 2 * tile_cols // THIRDS
    everything = tuple(range(THIRDS))

    slot_index = jnp.arange(own_cap, dtype=jnp.int32)
    block = jnp.where(slot_index < counts[0], grid_row // block_rows, n_row)
    earlier = (block[None, :] == block[:, None]) & (slot_index[None, :] < slot_index[:, None])
    rank = jnp.sum(earlier.astype(jnp.int32), axis=1)
    leaving = jnp.where(block < n_row, block * cap + rank, -1)
    hit = jnp.arange(slots, dtype=jnp.int32)[:, None] == leaving[None, :]
    spots = jnp.sum(jnp.where(hit, (grid_row % block_rows)[None, :] + 1, 0), axis=1) - 1
    picker = hit.astype(BF16)
    data = jnp.transpose(acq_data, (1, 0, 2))
    line = n_row <= 4 and block_rows == tile_cols
    my_row = lax.axis_index("row")
    labels = jnp.broadcast_to(spots.reshape(n_row, 1, cap), (n_row, n_col, cap))
    places = lax.all_to_all(
        labels.reshape(n_row * n_col, cap), ("row", "col"), split_axis=0, concat_axis=0, tiled=True
    ).reshape(-1)
    placer = (jnp.arange(block_rows, dtype=jnp.int32)[:, None] == places[None, :]).astype(BF16)

    tiles, lefts = [], []
    pair = None
    sent = [bin_rows(picker, data, f, n_row, n_col) for f in range(FREQ)]
    sent[0] = after(sent[0], places)
    for f in range(FREQ):
        got = lax.all_to_all(
            sent[f].reshape(n_row * n_col, cap, 2 * tile_cols), ("row", "col"), split_axis=0, concat_axis=0, tiled=True
        ).reshape(-1, 2 * tile_cols)
        if f == 0:
            got = after(got, sent[1])
        if pair is not None:
            got, pair, _ = lax.optimization_barrier((got, pair, lefts[0][0]))
        tile, *cut = place_rows(placer, got, (1,) * THIRDS if f else ())
        if line and f == 0:
            pair = hop((tile, tile), 1, n_row)
        tiles.append(tile)
        if f == 0:
            lefts.append((lax.all_gather(tile, "col", axis=0), everything))

    def gather_rows(part):
        if block_rows == tile_cols:
            return lax.all_gather(part, "row", axis=0)
        return lax.all_gather(part, "row", axis=1, tiled=True)

    sub = tile_cols // THIRDS
    views1 = [([(j, None)], 0) for j in everything]
    if line:
        right0, ups = [tiles[0], *pair], [0, 1, -1]
        second = pair
        for k in range(2, n_row):
            pair = hop(pair, k, n_row)
            second = pair if k == 2 else second
            right0 += list(pair)
            ups += [k, -k]
        cut = [after(part, pair if j else second) for j, part in enumerate(cut)]
    else:
        right0, ups = [gather_rows(tiles[0])], [None]
    right1 = [gather_rows(part) for part in cut]
    lefts.append((gather_cols(tiles[1], n_col, pair), everything))
    views0 = [(list(enumerate(ups)), j * sub) for j in everything]

    where = jnp.stack([my_row, lax.axis_index("col")]).astype(jnp.int32)
    product = functools.partial(complex_product, where)
    shape = (2, planes, block_rows, tile_cols)
    result, piece = product([lefts[0]], right0, views0, shape, (), (0, 0, 0))
    found = gather_cols(piece, n_col)
    result, most = product([lefts[1]], right1[:-1], views1[:-1], shape, (result,), (0, 1, 0))
    (result,) = product([(found, everything)], right0, views0, shape, (result,), (1, 0, 0))
    most = gather_cols(most, n_col, result)
    result, rest = product([lefts[1]], right1[-1:], views1[:1], shape, (result,), (0, 1, THIRDS - 1))
    most[0] = after(most[0], rest)
    (sums,) = product([(most, everything[:-1])], right1, views1, shape, (), None)
    rest = gather_cols(rest, n_col, sums)
    return product([(rest, everything[-1:])], right1, views1, shape, (result,), (1, 1, 0), before=sums)[0]


def solution(mesh):
    placed = (
        P(("groups", "row", "col"), None, None),
        P(("groups", "row", "col")),
        P(("groups", "row", "col")),
    )
    return jax.shard_map(
        per_device,
        mesh=mesh,
        in_specs=placed,
        out_specs=P("groups", None, "row", "col"),
        check_vma=False,
    )
```
